128 devices in a mesh: ctx: 32 (over z_hi, x, y), fsdp: 4 (over z_lo, core).
Axes of the slice: x: 4, y: 4, z: 4 (z_hi: 2, z_lo: 2; z = z_hi * 2 + z_lo), core: 2. Of those that a mesh axis runs over, the one named last changes fastest.
Arguments:
- tokens: bfloat16 [4, 4096, 960], P('fsdp', 'ctx'), may hold values from -6 to 6
- block_pairs: int32 [4, 32], P('fsdp'), may hold values from 0 to 31, each once within a row
- w_query: bfloat16 [960, 960], P('fsdp'), may hold values from -0.375 to 0.375
- key_weight: bfloat16 [960, 320], P('fsdp'), may hold values from -0.1875 to 0.1875
- value_weight: bfloat16 [960, 320], P('fsdp'), may hold values from -0.1875 to 0.1875
- w_out: bfloat16 [960, 960], P('fsdp'), may hold values from -0.75 to 0.75
- gain_attn: bfloat16 [960], P('fsdp'), may hold values from 0.25 to 1.75
- gain_mlp: bfloat16 [960], P('fsdp'), may hold values from 0.25 to 1.75
- w_gate: bfloat16 [960, 2560], P(None, 'fsdp'), may hold values from -0.1875 to 0.1875
- w_up: bfloat16 [960, 2560], P(None, 'fsdp'), may hold values from -0.1875 to 0.1875
- w_down: bfloat16 [2560, 960], P('fsdp'), may hold values from -0.25 to 0.25
- cotangent: bfloat16 [4, 4096, 960], P('fsdp', 'ctx'), may hold values from -6 to 6
Outputs:
- result: bfloat16 [4, 4096, 960], P('fsdp', 'ctx')
- input_grad: float32 [4, 4096, 960], P('fsdp', 'ctx')
- grad_query: float32 [960, 960], P('fsdp')
- grad_key: float32 [960, 320], P('fsdp')
- grad_value: float32 [960, 320], P('fsdp')
- grad_out: float32 [960, 960], P('fsdp')
- grad_gain_attn: float32 [960], P('fsdp')
- grad_gain_mlp: float32 [960], P('fsdp')
- grad_gate: float32 [960, 2560], P(None, 'fsdp')
- grad_up: float32 [960, 2560], P(None, 'fsdp')
- grad_down: float32 [2560, 960], P('fsdp')
The draws below stay inside these ranges and needn't reach their ends.
Inputs may be any that keep to these rules, and one draw needn't show every extreme that they name: Each row is a permutation; the index c of ctx holds, for that row's sequence, the position blocks block_pairs[s, c] and 63 - block_pairs[s, c], each of 64 positions, in that order.
All inputs are finite; a program needn't handle non-finite values.
Results may differ from the reference program's by a relative error of at most 0.03.
Values may be sent and summed in bfloat16 or wider, within the bound.
No kernel may reach another device: no remote copies, remote signals or barrier semaphores. Data moves between devices by JAX's collectives and lax.ppermute only.
A program may use at most 128 MiB of HBM per device.

```python
import jax
import jax.numpy as jnp
from jax import lax

MODEL_WIDTH = 960
FF = 2560
QUERY_HEADS = 15
KEY_VALUE_HEADS = 5
HEAD_SIZE = 64
HALF = 64
SEQUENCE_TOKENS = 4096
SEQS = 4
N_CTX = 32


def level_of(rng, extent, shards, smallest, high):
    gain, own = 1.0, jax.random.fold_in(rng, 6)
    for position, parts in shards:
        draws = jnp.exp(jax.random.uniform(jax.random.fold_in(own, position), (parts,), jnp.float32, smallest / len(shards), high / len(shards)))
        gain = gain * jnp.repeat(draws, extent[position] // parts).reshape([-1 if axis == position else 1 for axis in range(len(extent))])
    return gain


def noise(rng, dims, width, bound, shards=(), kind=jnp.bfloat16):
    gain = level_of(rng, dims, shards, -0.22, 0.18) if shards else 1.0
    entries = jax.random.normal(rng, dims, jnp.float32) * width * gain
    return jnp.minimum(jnp.maximum(entries, -bound), bound).astype(kind)


def setup_inputs(seed: int = 0) -> dict:
    seeds = jax.random.split(jax.random.key(seed), 13)
    tokens = noise(seeds[0], (SEQS, SEQUENCE_TOKENS, MODEL_WIDTH), 1.0, 6.0, ((0, 4), (1, 32)))
    block_pairs = jax.vmap(lambda own: jax.random.permutation(own, N_CTX))(jax.random.split(seeds[1], SEQS)).reshape((SEQS, N_CTX)).astype(jnp.int32)
    w_query = noise(seeds[2], (MODEL_WIDTH, QUERY_HEADS * HEAD_SIZE), (MODEL_WIDTH // 4) ** -0.5, 0.375, ((0, 4),))
    key_weight = noise(seeds[3], (MODEL_WIDTH, KEY_VALUE_HEADS * HEAD_SIZE), MODEL_WIDTH ** -0.5, 0.1875, ((0, 4),))
    value_weight = noise(seeds[4], (MODEL_WIDTH, KEY_VALUE_HEADS * HEAD_SIZE), MODEL_WIDTH ** -0.5, 0.1875, ((0, 4),))
    w_out = noise(seeds[5], (QUERY_HEADS * HEAD_SIZE, MODEL_WIDTH), (QUERY_HEADS * HEAD_SIZE // 16) ** -0.5, 0.75, ((0, 4),))
    gain_attn = jnp.clip(1.0 + 0.15 * jax.random.normal(seeds[6], (MODEL_WIDTH,), jnp.float32), 0.25, 1.75).astype(jnp.bfloat16)
    gain_mlp = jnp.clip(1.0 + 0.15 * jax.random.normal(seeds[7], (MODEL_WIDTH,), jnp.float32), 0.25, 1.75).astype(jnp.bfloat16)
    w_gate = noise(seeds[8], (MODEL_WIDTH, FF), MODEL_WIDTH ** -0.5, 0.1875, ((1, 4),))
    w_up = noise(seeds[9], (MODEL_WIDTH, FF), MODEL_WIDTH ** -0.5, 0.1875, ((1, 4),))
    w_down = noise(seeds[10], (FF, MODEL_WIDTH), (FF // 4) ** -0.5, 0.25, ((0, 4),))
    cotangent = noise(seeds[11], (SEQS, SEQUENCE_TOKENS, MODEL_WIDTH), 1.0, 6.0, ((0, 4), (1, 32)))
    return dict(tokens=tokens, block_pairs=block_pairs, w_query=w_query, key_weight=key_weight, value_weight=value_weight, w_out=w_out, gain_attn=gain_attn, gain_mlp=gain_mlp, w_gate=w_gate, w_up=w_up, w_down=w_down, cotangent=cotangent)


@jax.custom_vjp
def reduced_precision(v):
    return lax.optimization_barrier(v.astype(jnp.bfloat16)).astype(jnp.float32)

@jax.custom_vjp
def reduced_precision_back(v):
    return v

def low_keep(v):
    return (reduced_precision(v), None)

def low_pass(kept, grad):
    return (grad,)

def back_keep(v):
    return (v, None)

def back_low(kept, grad):
    return (reduced_precision(grad),)
reduced_precision.defvjp(low_keep, low_pass)
reduced_precision_back.defvjp(back_keep, back_low)
EPSILON = 1e-05
HIGHEST = lax.Precision.HIGHEST

def product_result(left, right):
    return jnp.dot(left, right, precision=HIGHEST, preferred_element_type=jnp.float32)

def rms_norm(values, gain_vector):
    return values * lax.rsqrt(lax.optimization_barrier(jnp.mean(values * values, axis=-1, keepdims=True)) + EPSILON) * gain_vector

def apply_rotation(values, cosine_table, sinusoid_table):
    half_width = values.shape[-1] // 2
    leading = values[..., :half_width]
    trailing = values[..., half_width:]
    return jnp.concatenate([leading * cosine_table - trailing * sinusoid_table, trailing * cosine_table + leading * sinusoid_table], axis=-1)

def positions(pair_row):
    block_list = jnp.stack([pair_row, 2 * N_CTX - 1 - pair_row], axis=1).astype(jnp.int32)
    offsets = jnp.arange(HALF, dtype=jnp.int32)
    return (block_list[:, :, None] * HALF + offsets[None, None, :]).reshape(-1).astype(jnp.int32)

def full_layer(inputs, block_locations, weights):
    w_query, key_weight, value_weight, w_out, gain_attn, gain_mlp, w_gate, w_up, w_down = weights
    query_group_width = QUERY_HEADS // KEY_VALUE_HEADS
    frequency = 10000.0 ** (-jnp.arange(HEAD_SIZE // 2, dtype=jnp.float32) / (HEAD_SIZE // 2))
    angles = block_locations.astype(jnp.float32)[:, None] * frequency[None, :]
    cosine_table = jnp.cos(angles)[:, None, :]
    sinusoid_table = jnp.sin(angles)[:, None, :]
    normalized_input = reduced_precision(rms_norm(inputs, gain_attn))
    query_matrix = reduced_precision(apply_rotation(reduced_precision_back(product_result(normalized_input, w_query)).reshape(SEQUENCE_TOKENS, QUERY_HEADS, HEAD_SIZE), cosine_table, sinusoid_table))
    rows_of_key = reduced_precision(apply_rotation(reduced_precision_back(product_result(normalized_input, key_weight)).reshape(SEQUENCE_TOKENS, KEY_VALUE_HEADS, HEAD_SIZE), cosine_table, sinusoid_table))
    rows_of_value = reduced_precision(reduced_precision_back(product_result(normalized_input, value_weight))).reshape(SEQUENCE_TOKENS, KEY_VALUE_HEADS, HEAD_SIZE)
    factor = HEAD_SIZE ** (-0.5)
    rows_per_block = min(512, SEQUENCE_TOKENS)

    def attend_pair(block_item):
        query_block, query_places = block_item
        scores = jnp.einsum('qkgd,skd->kgqs', query_block, rows_of_key, precision=HIGHEST) * factor
        allowed = query_places[:, None] >= block_locations[None, :]
        scores = reduced_precision_back(jnp.where(allowed[None, None], scores, -1e+30))
        soft_weights = jax.nn.softmax(scores, axis=-1)
        return jnp.einsum('kgqs,skd->qkgd', reduced_precision(soft_weights), rows_of_value, precision=HIGHEST)
    block_list = lax.map(jax.checkpoint(attend_pair), (query_matrix.reshape(SEQUENCE_TOKENS // rows_per_block, rows_per_block, KEY_VALUE_HEADS, query_group_width, HEAD_SIZE), block_locations.reshape(SEQUENCE_TOKENS // rows_per_block, rows_per_block)))
    attended = reduced_precision(reduced_precision_back(block_list.reshape(SEQUENCE_TOKENS, QUERY_HEADS * HEAD_SIZE)))
    middle = inputs + reduced_precision_back(product_result(attended, w_out))
    normed_mlp = reduced_precision(rms_norm(middle, gain_mlp))
    gate_pre = reduced_precision_back(product_result(normed_mlp, w_gate))
    up_pre = reduced_precision_back(product_result(normed_mlp, w_up))
    hidden = reduced_precision(jax.nn.silu(gate_pre) * up_pre)
    return middle + reduced_precision_back(product_result(hidden, w_down))

def reference(tokens, block_pairs, w_query, key_weight, value_weight, w_out, gain_attn, gain_mlp, w_gate, w_up, w_down, cotangent):
    weights = tuple((tensor.astype(jnp.float32) for tensor in (w_query, key_weight, value_weight, w_out, gain_attn, gain_mlp, w_gate, w_up, w_down)))

    def per_sequence(running, sequence):
        seq_tokens, seq_cotangent, pair_row = sequence
        block_locations = positions(pair_row)
        outputs, pullback = jax.vjp(lambda inputs, params: full_layer(inputs, block_locations, params), seq_tokens.astype(jnp.float32), weights)
        input_part, weight_parts = pullback(seq_cotangent.astype(jnp.float32))
        running = tuple((before + increment for before, increment in zip(running, weight_parts)))
        return (running, (outputs.astype(jnp.bfloat16), input_part))
    zeros = tuple((jnp.zeros_like(tensor) for tensor in weights))
    totals, (outputs, input_grads) = lax.scan(per_sequence, zeros, (tokens, cotangent, block_pairs))
    return (outputs, input_grads, totals[0], totals[1], totals[2], totals[3], totals[4], totals[5], totals[6], totals[7], totals[8])
```

```python
import jax
import jax.numpy as jnp
from jax import lax
from jax.sharding import Mesh, PartitionSpec as P

QUERY_HEADS = 15
KEY_VALUE_HEADS = 5
HEAD_SIZE = 64
EPSILON = 1e-05
BF = jnp.bfloat16
F32 = jnp.float32
FS = ("zl", "co")
RING = (0, -1, 1, 2)


def matrix_product(left, right):
    return jnp.dot(left, right, preferred_element_type=F32)


def left_inner(left, right):
    return lax.dot_general(left, right, (((0,), (0,)), ((), ())), preferred_element_type=F32)


def right_inner(left, right):
    return lax.dot_general(left, right, (((1,), (1,)), ((), ())), preferred_element_type=F32)


def shift(value, axis, step):
    count = lax.axis_size(axis)
    return lax.ppermute(value, axis, [(i, (i + step) % count) for i in range(count)])


def ring_gather(value, axis):
    half = value.shape[0] // 2
    left = shift(value, axis, 1)
    right = shift(value, axis, -1)
    far_one = shift(left[:half], axis, 1)
    far_two = shift(right[half:], axis, -1)
    return jnp.concatenate([value, left, right, far_one, far_two], axis=0)


def add_low(*parts):
    total = parts[0].astype(F32)
    for part in parts[1:]:
        total = total + part.astype(F32)
    return total.astype(BF)


def ring_scatter(value, axis):
    rows = value.shape[0] // 4
    half = rows // 2
    own, left, right = value[:rows], value[rows : 2 * rows], value[2 * rows : 3 * rows]
    from_left = shift(value[3 * rows : 3 * rows + half], axis, 1)
    from_right = shift(value[3 * rows + half :], axis, -1)
    right = jnp.concatenate([add_low(right[:half], from_left), right[half:]], axis=0)
    left = jnp.concatenate([left[:half], add_low(left[half:], from_right)], axis=0)
    return add_low(own, shift(right, axis, 1), shift(left, axis, -1))


def ring_pick(value, axis):
    here = lax.axis_index(axis)
    return jnp.concatenate(
        [lax.dynamic_slice_in_dim(value, lax.rem(here + off + 4, 4), 1, axis=0) for off in RING], axis=0
    )


def ring_place(value, axis):
    here = lax.axis_index(axis)
    out = value
    for place, off in enumerate(RING):
        out = lax.dynamic_update_slice_in_dim(
            out, value[place : place + 1], lax.rem(here + off + 4, 4), axis=0
        )
    return out


def pair_gather(value):
    both = jnp.concatenate([value[None], shift(value, "zl", 1)[None]], axis=0)
    other = shift(both, "co", 1)
    return jnp.stack([both[0], other[0], both[1], other[1]])


def pair_scatter(value):
    near = add_low(value[:2], shift(value[2:].astype(BF), "zl", 1))
    return near[0].astype(F32) + shift(near[1], "co", 1).astype(F32)


def weight_gather(value):
    rows = value.shape[0]
    cut = 128
    zed = ("zh", "zl")
    one = shift(value[:cut], zed, 1)
    two = shift(value[cut:], zed, -1)
    core = shift(value, "co", 1)
    core_one = shift(one, "co", 1)
    core_two = shift(two, "co", 1)
    place = 2 * lax.axis_index("zl") + lax.axis_index("co")
    out = jnp.zeros((4, rows) + value.shape[1:], value.dtype)
    for mask, block in (
        (0, value),
        (1, core),
        (2, jnp.concatenate([one, two], axis=0)),
        (3, jnp.concatenate([core_one, core_two], axis=0)),
    ):
        out = lax.dynamic_update_slice_in_dim(out, block[None], place ^ mask, axis=0)
    return out.reshape((4 * rows,) + value.shape[1:])


def direct_scatter(value, axis):
    near = [shift(value[place], axis, off) for place, off in ((1, -1), (2, 1), (3, 2))]
    return add_low(value[0], *near)


def direct_gather(value, axis):
    return jnp.stack([value, shift(value, axis, 1), shift(value, axis, -1), shift(value, axis, 2)])


def wide_gather(value, axis):
    left = shift(value, axis, 1)
    right = shift(value, axis, -1)
    far_one = shift(left[:, :2], axis, 1)
    far_two = shift(right[:, 2:], axis, -1)
    return jnp.concatenate([value, left, right, jnp.concatenate([far_one, far_two], axis=1)], axis=0)


def wide_scatter(value, axis):
    own, left, right = value[0], value[1], value[2]
    half = own.shape[0] // 2
    from_left = shift(value[3, :half], axis, 1)
    from_right = shift(value[3, half:], axis, -1)
    right = jnp.concatenate([add_low(right[:half], from_left), right[half:]], axis=0)
    left = jnp.concatenate([left[:half], add_low(left[half:], from_right)], axis=0)
    return add_low(own, shift(right, axis, 1), shift(left, axis, -1))


def reduce_sum(value, first, second):
    shape = value.shape
    out = value.reshape((4, 4) + shape[1:])
    out = wide_scatter(ring_pick(out, first), first)
    out = direct_scatter(ring_pick(out, second), second)
    out = add_low(out, shift(out, "zh", 1))
    out = ring_place(direct_gather(out, second), second)[None]
    out = ring_place(wide_gather(out, first), first)
    return out.reshape(shape)


def context_gather(value, first, second):
    out = jnp.stack([value, shift(value, "zh", 1)])
    return ring_gather(ring_gather(out, first), second)


def context_scatter(value, first, second):
    out = ring_scatter(ring_scatter(value, second), first)
    return out[0].astype(F32) + shift(out[1], "zh", 1).astype(F32)


def swap_order(value):
    return jnp.swapaxes(value.reshape((4, 4, 2) + value.shape[1:]), 0, 1).reshape(value.shape)


def apply_rotation(values, cosine_table, sinusoid_table):
    half = values.shape[-1] // 2
    leading, trailing = values[..., :half], values[..., half:]
    return jnp.concatenate(
        [
            leading * cosine_table - trailing * sinusoid_table,
            trailing * cosine_table + leading * sinusoid_table,
        ],
        axis=-1,
    )


def norm_forward(values, gain_vector):
    inverse = lax.rsqrt(jnp.mean(values * values, axis=-1, keepdims=True) + EPSILON)
    return (values * inverse * gain_vector, inverse)


def norm_backward(values, inverse, gain_vector, gradient):
    weighted = gradient * gain_vector
    through = inverse * weighted - values * inverse**3 * jnp.mean(
        weighted * values, axis=-1, keepdims=True
    )
    return (through, jnp.sum(gradient * values * inverse, axis=0))


def pair_positions(pair_rows, count, span):
    block_list = jnp.stack([pair_rows, 2 * count - 1 - pair_rows], axis=-1)
    offsets = jnp.arange(span, dtype=jnp.int32)
    return (block_list[..., None] * span + offsets).reshape(-1)


def masked_scores(query_rows, key_block, query_places, key_places, factor):
    scores = (
        jnp.einsum("qkgd,skd->kgqs", query_rows, key_block, preferred_element_type=F32) * factor
    )
    allowed = query_places[:, None] >= key_places[None, :]
    return jnp.where(allowed[None, None], scores, -1e30)


def split_blocks(rows_of_key, rows_of_value, key_places):
    return (
        rows_of_key.reshape((8, 512) + rows_of_key.shape[1:]),
        rows_of_value.reshape((8, 512) + rows_of_value.shape[1:]),
        key_places.reshape(8, 512),
    )


def attention_forward(query_rows, rows_of_key, rows_of_value, query_places, key_places, factor):
    blocks = split_blocks(rows_of_key, rows_of_value, key_places)
    shape_stat = (query_rows.shape[1], query_rows.shape[2], query_rows.shape[0])

    def statistics(running, block_item):
        running_max, running_sum = running
        key_block, _, key_place = block_item
        scores = masked_scores(query_rows, key_block, query_places, key_place, factor)
        new_max = jnp.maximum(running_max, jnp.max(scores, axis=-1))
        running_sum = running_sum * jnp.exp(running_max - new_max) + jnp.sum(
            jnp.exp(scores - new_max[..., None]), axis=-1
        )
        return ((new_max, running_sum), None)

    (row_max, row_sum), _ = lax.scan(
        statistics, (jnp.full(shape_stat, -1e30, F32), jnp.zeros(shape_stat, F32)), blocks
    )
    log_total = row_max + jnp.log(row_sum)

    def accumulate(running, block_item):
        key_block, value_block, key_place = block_item
        scores = masked_scores(query_rows, key_block, query_places, key_place, factor)
        soft_weights = jnp.exp(scores - log_total[..., None]).astype(BF)
        return (
            running
            + jnp.einsum("kgqs,skd->qkgd", soft_weights, value_block, preferred_element_type=F32),
            None,
        )

    attended, _ = lax.scan(accumulate, jnp.zeros(query_rows.shape, F32), blocks)
    return (attended, log_total)


def attention_backward(
    query_rows, rows_of_key, rows_of_value, query_places, key_places, factor, attended, log_total, attended_gradient
):
    blocks = split_blocks(rows_of_key, rows_of_value, key_places)
    row_delta = jnp.transpose(
        jnp.sum(attended_gradient.astype(F32) * attended, axis=-1), (1, 2, 0)
    )

    def backward_block(running, block_item):
        key_block, value_block, key_place = block_item
        scores = masked_scores(query_rows, key_block, query_places, key_place, factor)
        soft_weights = jnp.exp(scores - log_total[..., None])
        grad_soft = jnp.einsum(
            "qkgd,skd->kgqs", attended_gradient, value_block, preferred_element_type=F32
        )
        grad_scores = (soft_weights * (grad_soft - row_delta[..., None])).astype(BF)
        running = running + jnp.einsum(
            "kgqs,skd->qkgd", grad_scores, key_block, preferred_element_type=F32
        )
        grad_key_block = (
            jnp.einsum("kgqs,qkgd->skd", grad_scores, query_rows, preferred_element_type=F32) * factor
        ).astype(BF)
        grad_value_block = jnp.einsum(
            "kgqs,qkgd->skd", soft_weights.astype(BF), attended_gradient, preferred_element_type=F32
        ).astype(BF)
        return (running, (grad_key_block, grad_value_block))

    grad_queries, (grad_key_rows, grad_value_rows) = lax.scan(
        backward_block, jnp.zeros(query_rows.shape, F32), blocks
    )
    return (grad_queries * factor, grad_key_rows, grad_value_rows)


def body(
    tokens, block_pairs, w_query, key_weight, value_weight, w_out, gain_attn, gain_mlp, w_gate, w_up, w_down, cotangent
):
    rows, width = tokens.shape[1:]
    kv_width = KEY_VALUE_HEADS * HEAD_SIZE
    factor = HEAD_SIZE ** (-0.5)
    x_here, y_here, z_here = lax.axis_index("x"), lax.axis_index("y"), lax.axis_index("zh")
    place = 2 * lax.axis_index("zl") + lax.axis_index("co")
    context = z_here * 16 + x_here * 4 + y_here

    weights_in = weight_gather(jnp.concatenate([w_query, key_weight, value_weight], axis=1))
    out_w = weight_gather(w_out)
    gains = lax.all_gather(jnp.stack([gain_attn, gain_mlp])[None], FS, axis=0, tiled=True)
    gains = jnp.swapaxes(gains, 0, 1).reshape(2, width).astype(F32)
    gain_one, gain_two = gains[0], gains[1]

    inputs = tokens[0].astype(F32)
    upstream = cotangent[0].astype(F32)
    grad_mlp = pair_gather(cotangent[0]).reshape(4 * rows, width)

    order = [
        ((z_here + z) % 2) * 16 + ((x_here + x + 4) % 4) * 4 + (y_here + y + 4) % 4
        for x in RING
        for y in RING
        for z in (0, 1)
    ]
    pairs = block_pairs[0][jnp.stack(order)]
    query_places = pair_positions(pairs[:1], 32, rows // 2)
    key_places = pair_positions(pairs, 32, rows // 2)
    frequency = 10000.0 ** (-jnp.arange(HEAD_SIZE // 2, dtype=F32) / (HEAD_SIZE // 2))
    angles = query_places.astype(F32)[:, None] * frequency[None, :]
    cosine_table, sinusoid_table = jnp.cos(angles)[:, None, :], jnp.sin(angles)[:, None, :]

    normed_one, inverse_one = norm_forward(inputs, gain_one)
    normed_low = normed_one.astype(BF)
    projected = matrix_product(normed_low, weights_in)
    heads = QUERY_HEADS + KEY_VALUE_HEADS
    rotated = apply_rotation(
        projected[:, : width + kv_width].reshape(rows, heads, HEAD_SIZE), cosine_table, sinusoid_table
    ).astype(BF)
    queries = rotated[:, :QUERY_HEADS]
    keys = rotated[:, QUERY_HEADS:].reshape(rows, kv_width)
    values = projected[:, width + kv_width :].astype(BF)

    all_keys = context_gather(keys, "y", "x")
    all_values = swap_order(context_gather(values, "x", "y"))
    grouped = queries.reshape(rows, KEY_VALUE_HEADS, -1, HEAD_SIZE)
    heads_of_key = all_keys.reshape(-1, KEY_VALUE_HEADS, HEAD_SIZE)
    heads_of_value = all_values.reshape(-1, KEY_VALUE_HEADS, HEAD_SIZE)
    attended, log_total = attention_forward(
        grouped, heads_of_key, heads_of_value, query_places, key_places, factor
    )
    attended_low = attended.reshape(rows, width).astype(BF)
    middle = inputs + matrix_product(attended_low, out_w)
    normed_two, inverse_two = norm_forward(middle, gain_two)
    normed_mlp = pair_gather(normed_two.astype(BF)).reshape(4 * rows, width)

    gate_pre = matrix_product(normed_mlp, w_gate)
    up_pre = matrix_product(normed_mlp, w_up)
    grad_hidden = right_inner(grad_mlp, w_down)
    sigmoid_gate = jax.nn.sigmoid(gate_pre)
    hidden = (gate_pre * sigmoid_gate * up_pre).astype(BF)
    grad_up_pre = (grad_hidden * gate_pre * sigmoid_gate).astype(BF)
    grad_gate_pre = (
        grad_hidden * up_pre * sigmoid_gate * (1.0 + gate_pre * (1.0 - sigmoid_gate))
    ).astype(BF)
    grad_normed_two = right_inner(grad_gate_pre, w_gate) + right_inner(grad_up_pre, w_up)
    grad_normed_two = pair_scatter(grad_normed_two.astype(BF).reshape(4, rows, width))
    mlp_term = pair_scatter(matrix_product(hidden, w_down).astype(BF).reshape(4, rows, width))
    result = (middle + mlp_term).astype(BF)[None]

    pad = ((0, 64), (0, 0))
    grad_gate_w = jnp.pad(left_inner(normed_mlp, grad_gate_pre).astype(BF), pad).reshape(16, 64, -1)
    grad_up_w = jnp.pad(left_inner(normed_mlp, grad_up_pre).astype(BF), pad).reshape(16, 64, -1)
    grad_down_w = jnp.pad(left_inner(grad_mlp, hidden).astype(BF), pad).reshape(2, 16, 32, -1)
    sum_one = reduce_sum(jnp.concatenate([grad_gate_w, grad_down_w[0]], axis=1), "x", "y")
    sum_two = reduce_sum(jnp.concatenate([grad_up_w, grad_down_w[1]], axis=1), "y", "x")

    through_two, grad_gain_two = norm_backward(middle, inverse_two, gain_two, grad_normed_two)
    grad_middle = upstream + through_two
    grad_branch = grad_middle.astype(BF)
    attended_gradient = right_inner(grad_branch, out_w).astype(BF)
    grad_queries, key_gradients, value_gradients = attention_backward(
        grouped,
        heads_of_key,
        heads_of_value,
        query_places,
        key_places,
        factor,
        attended,
        log_total,
        attended_gradient.reshape(grouped.shape),
    )
    own_key_gradient = context_scatter(key_gradients.reshape(32, rows, kv_width), "y", "x")
    own_value_gradient = context_scatter(
        swap_order(value_gradients.reshape(32, rows, kv_width)), "x", "y"
    )
    grad_query_pre = (
        apply_rotation(grad_queries.reshape(rows, QUERY_HEADS, HEAD_SIZE), cosine_table, -sinusoid_table)
        .reshape(rows, width)
        .astype(BF)
    )
    grad_key_pre = (
        apply_rotation(
            own_key_gradient.reshape(rows, KEY_VALUE_HEADS, HEAD_SIZE), cosine_table, -sinusoid_table
        )
        .reshape(rows, kv_width)
        .astype(BF)
    )
    grad_kv = jnp.concatenate([grad_key_pre, own_value_gradient.astype(BF)], axis=1)

    def own_columns(value):
        blocks = value.T.reshape(4, width // 4, rows)
        parts = []
        for mask in range(4):
            part = lax.dynamic_index_in_dim(blocks, place ^ mask, axis=0, keepdims=False)
            if mask:
                part = lax.ppermute(part, FS, [(i, i ^ mask) for i in range(4)])
            parts.append(part)
        return jnp.concatenate(parts, axis=1)

    normed_columns = own_columns(normed_low)
    attended_columns = own_columns(attended_low)
    all_branch = pair_gather(grad_branch).reshape(4 * rows, width)
    all_query = pair_gather(grad_query_pre).reshape(4 * rows, width)
    all_kv = pair_gather(grad_kv).reshape(4 * rows, 2 * kv_width)
    pad = ((0, 16), (0, 0))
    grad_out_w = jnp.pad(matrix_product(attended_columns, all_branch).astype(BF), pad)
    grad_query_w = jnp.pad(matrix_product(normed_columns, all_query).astype(BF), pad)
    sum_out = reduce_sum(grad_out_w.reshape(16, 16, width), "x", "y")
    sum_query = reduce_sum(grad_query_w.reshape(16, 16, width), "y", "x")

    grad_kv_w = matrix_product(normed_columns, all_kv).astype(BF)
    grad_normed_one = right_inner(jnp.concatenate([grad_query_pre, grad_kv], axis=1), weights_in)
    through_one, grad_gain_one = norm_backward(inputs, inverse_one, gain_one, grad_normed_one)
    input_grad = (grad_middle + through_one)[None]

    grad_gains = jnp.stack([grad_gain_one, grad_gain_two]).astype(BF)
    grad_gains = lax.psum(grad_gains, FS)
    grad_gains = lax.dynamic_slice_in_dim(grad_gains, place * (width // 4), width // 4, axis=1)
    last = jnp.concatenate(
        [grad_kv_w, jnp.pad(grad_gains, ((0, 14), (0, 2 * kv_width - width // 4)))], axis=0
    )
    sum_last = reduce_sum(last.reshape(16, 16, 2 * kv_width), "x", "y").reshape(256, 2 * kv_width)

    quarter = width // 4
    hidden_shard = w_gate.shape[1]
    sum_down = jnp.concatenate(
        [sum_one[:, 64:].reshape(512, hidden_shard), sum_two[:, 64:].reshape(512, hidden_shard)], axis=0
    )[:width]
    return (
        result,
        input_grad,
        sum_query.reshape(256, width)[:quarter].astype(F32),
        sum_last[:quarter, :kv_width].astype(F32),
        sum_last[:quarter, kv_width:].astype(F32),
        sum_out.reshape(256, width)[:quarter].astype(F32),
        sum_last[quarter, :quarter].astype(F32),
        sum_last[quarter + 1, :quarter].astype(F32),
        sum_one[:, :64].reshape(1024, hidden_shard)[:width].astype(F32),
        sum_two[:, :64].reshape(1024, hidden_shard)[:width].astype(F32),
        sum_down.T.astype(F32),
    )


def solution(mesh):
    split = Mesh(mesh.devices.reshape(2, 4, 4, 2, 2), ("zh", "x", "y", "zl", "co"))
    ctx = ("zh", "x", "y")
    in_specs = (
        P(FS, ctx, None),
        P(FS, None),
        P(FS, None),
        P(FS, None),
        P(FS, None),
        P(FS, None),
        P(FS),
        P(FS),
        P(None, FS),
        P(None, FS),
        P(FS, None),
        P(FS, ctx, None),
    )
    out_specs = (
        P(FS, ctx, None),
        P(FS, ctx, None),
        P(FS, None),
        P(FS, None),
        P(FS, None),
        P(FS, None),
        P(FS),
        P(FS),
        P(None, FS),
        P(None, FS),
        P(FS, None),
    )
    return jax.shard_map(body, mesh=split, in_specs=in_specs, out_specs=out_specs, check_vma=False)
```

```python
import functools

import jax
import jax.numpy as jnp
from jax import lax
from jax.experimental import pallas as pl
from jax.experimental.pallas import tpu as pltpu
from jax.sharding import Mesh, PartitionSpec as P

QUERY_HEADS = 15
KEY_VALUE_HEADS = 5
HEAD_SIZE = 64
EPSILON = 1e-05
BF = jnp.bfloat16
F32 = jnp.float32
FS = ("zl", "co")
RING = (0, -1, 1, 2)


def matrix_product(left, right):
    return jnp.dot(left, right, preferred_element_type=F32)


def left_inner(left, right):
    return lax.dot_general(left, right, (((0,), (0,)), ((), ())), preferred_element_type=F32)


def right_inner(left, right):
    return lax.dot_general(left, right, (((1,), (1,)), ((), ())), preferred_element_type=F32)


def shift(value, axis, step):
    count = lax.axis_size(axis)
    return lax.ppermute(value, axis, [(i, (i + step) % count) for i in range(count)])


def add_low(*parts):
    total = parts[0].astype(F32)
    for part in parts[1:]:
        total = total + part.astype(F32)
    return total.astype(BF)


def together(*values):
    return lax.optimization_barrier(values)


def ring_pick(value, axis):
    here = lax.axis_index(axis)
    return [
        lax.dynamic_index_in_dim(value, lax.rem(here + off + 4, 4), axis=0, keepdims=False) for off in RING
    ]


def ring_place(blocks, axis):
    here = lax.axis_index(axis)
    out = jnp.stack(blocks)
    for block, off in zip(blocks, RING):
        out = lax.dynamic_update_slice_in_dim(out, block[None], lax.rem(here + off + 4, 4), axis=0)
    return out


def near_gather(value, axis):
    return [value, shift(value, axis, 1), shift(value, axis, -1), shift(value, axis, 2)]


def near_scatter(blocks, axis):
    return [blocks[0], shift(blocks[1], axis, -1), shift(blocks[2], axis, 1), shift(blocks[3], axis, 2)]


def two_ring_gather(one, two, axis_one, axis_two):
    left_one, right_one, left_two, right_two = together(
        shift(one, axis_one, 1), shift(one, axis_one, -1), shift(two, axis_two, 1), shift(two, axis_two, -1)
    )
    half = one.shape[0] // 2
    far = together(
        shift(left_one[:half], axis_one, 1),
        shift(right_one[half:], axis_one, -1),
        shift(left_two[:half], axis_two, 1),
        shift(right_two[half:], axis_two, -1),
    )
    return (one, left_one, right_one, far[0], far[1]), (two, left_two, right_two, far[2], far[3])


def ring_far(one, two, axis_one, axis_two):
    return together(
        shift(one[3], axis_one, 1), shift(one[4], axis_one, -1), shift(two[3], axis_two, 1), shift(two[4], axis_two, -1)
    )


def ring_near(one, two, far, axis_one, axis_two):
    sends = []
    for pieces, from_left, from_right in ((one, far[0], far[1]), (two, far[2], far[3])):
        half = from_left.shape[0]
        right, left = pieces[2], pieces[1]
        sends.append(jnp.concatenate([add_low(right[:half], from_left), right[half:]], axis=0))
        sends.append(jnp.concatenate([left[:half], add_low(left[half:], from_right)], axis=0))
    got = together(
        shift(sends[0], axis_one, 1),
        shift(sends[1], axis_one, -1),
        shift(sends[2], axis_two, 1),
        shift(sends[3], axis_two, -1),
    )
    return add_low(one[0], got[0], got[1]), add_low(two[0], got[2], got[3])


def pair_gather(value):
    both = jnp.concatenate([value[None], shift(value, "zl", 1)[None]], axis=0)
    other = shift(both, "co", 1)
    return jnp.stack([both[0], other[0], both[1], other[1]])


def pair_scatter(value):
    near = add_low(value[:2], shift(value[2:].astype(BF), "zl", 1))
    return near[0].astype(F32) + shift(near[1], "co", 1).astype(F32)


def weight_gather(value):
    rows = value.shape[0]
    cut = 128
    zed = ("zh", "zl")
    one = shift(value[:cut], zed, 1)
    two = shift(value[cut:], zed, -1)
    core = shift(value, "co", 1)
    core_one = shift(one, "co", 1)
    core_two = shift(two, "co", 1)
    place = 2 * lax.axis_index("zl") + lax.axis_index("co")
    out = jnp.zeros((4, rows) + value.shape[1:], value.dtype)
    for mask, block in (
        (0, value),
        (1, core),
        (2, jnp.concatenate([one, two], axis=0)),
        (3, jnp.concatenate([core_one, core_two], axis=0)),
    ):
        out = lax.dynamic_update_slice_in_dim(out, block[None], place ^ mask, axis=0)
    return out.reshape((4 * rows,) + value.shape[1:])


def context_gather(keys, values):
    width = keys.shape[1]
    both = jnp.concatenate([keys, values], axis=1)
    other = shift(both, "zh", 1)
    keys = jnp.stack([keys, other[:, :width]])
    values = jnp.stack([values, other[:, width:]])
    near = together(*near_gather(keys, "y"), *near_gather(values, "x"))
    return two_ring_gather(jnp.concatenate(near[:4]), jnp.concatenate(near[4:]), "x", "y")


def context_scatter(keys, values):
    keys, values = ring_near(keys, values, ring_far(keys, values, "x", "y"), "x", "y")
    keys = [keys[2 * place : 2 * place + 2] for place in range(4)]
    values = [values[2 * place : 2 * place + 2] for place in range(4)]
    near = together(*near_scatter(keys, "y"), *near_scatter(values, "x"))
    keys, values = add_low(*near[:4]), add_low(*near[4:])
    other = shift(jnp.concatenate([keys[1], values[1]], axis=1), "zh", 1).astype(F32)
    width = keys.shape[-1]
    return keys[0].astype(F32) + other[:, :width], values[0].astype(F32) + other[:, width:]


def column_exchange(value, place):
    mine = lax.dynamic_index_in_dim(value, place, axis=0, keepdims=False)
    parts = [mine] + [
        lax.dynamic_index_in_dim(value, place ^ mask, axis=0, keepdims=False) for mask in (1, 2, 3)
    ]
    from_z = shift(jnp.stack(parts[2:]), "zl", 1)
    from_core = shift(jnp.stack([parts[1], from_z[1]]), "co", 1)
    return jnp.concatenate([mine, from_core[0], from_z[0], from_core[1]], axis=-1)


def apply_rotation(values, cosine_table, sinusoid_table):
    half = values.shape[-1] // 2
    leading, trailing = values[..., :half], values[..., half:]
    return jnp.concatenate(
        [
            leading * cosine_table - trailing * sinusoid_table,
            trailing * cosine_table + leading * sinusoid_table,
        ],
        axis=-1,
    )


def norm_forward(values, gain_vector):
    inverse = lax.rsqrt(jnp.mean(values * values, axis=-1, keepdims=True) + EPSILON)
    return (values * inverse * gain_vector, inverse)


def norm_backward(values, inverse, gain_vector, gradient):
    weighted = gradient * gain_vector
    through = inverse * weighted - values * inverse**3 * jnp.mean(
        weighted * values, axis=-1, keepdims=True
    )
    return (through, jnp.sum(gradient * values * inverse, axis=0))


HEAD_GROUPS = ((0, 2), (1, 2), (2, 1))
NEGATIVE = -1e30


def nt(left, right):
    return lax.dot_general(left, right, (((1,), (1,)), ((), ())), preferred_element_type=F32)


def tn(left, right):
    return lax.dot_general(left, right, (((0,), (0,)), ((), ())), preferred_element_type=F32)


def swap_halves(slab):
    return jnp.concatenate([slab[:, 64:], slab[:, :64]], axis=1)


def spread_heads(rows, kv_heads):
    lane = lax.broadcasted_iota(jnp.int32, (64, 128), 1)
    blocks = []
    for kv in range(kv_heads):
        for group in range(3):
            head = 3 * kv + group
            slab = rows[:, 128 * (head // 2) : 128 * (head // 2) + 128]
            if head % 2 != kv:
                slab = swap_halves(slab)
            blocks.append(jnp.where((lane < 64) == (kv == 0), slab, 0.0))
    return jnp.concatenate(blocks, axis=0)


def unspread_heads(blocks, kv_heads):
    lane = lax.broadcasted_iota(jnp.int32, (64, 128), 1)
    count = 3 * kv_heads
    slabs = []
    for slab in range((count + 1) // 2):
        halves = []
        for side in range(2):
            head = 2 * slab + side
            if head >= count:
                halves.append(jnp.zeros((64, 128), F32))
                continue
            block = blocks[64 * head : 64 * head + 64]
            halves.append(block if head // 3 == side else swap_halves(block))
        slabs.append(jnp.where(lane < 64, halves[0], halves[1]))
    return jnp.concatenate(slabs, axis=1)


def causal_mask(columns):
    key = lax.broadcasted_iota(jnp.int32, (64, columns), 0)
    query = lax.rem(lax.broadcasted_iota(jnp.int32, (64, columns), 1), 64)
    return key <= query


def fill_chunks(pieces, low, high, outer_first, start, width):
    if width % 128:
        zeros = jnp.zeros((2048, 64), BF)
        low[:, width : width + 64] = zeros
        high[:, width : width + 64] = zeros
    for chunk in range(32):
        one, two, zed = chunk // 8, (chunk // 2) % 4, chunk % 2
        outer, inner = (one, two) if outer_first else (two, one)
        if outer < 3:
            block = pieces[outer].at[2 * inner + zed]
        else:
            block = pieces[3 + inner // 2].at[2 * (inner % 2) + zed]
        low[64 * chunk : 64 * chunk + 64, 0:width] = block[0:64, start : start + width]
        high[64 * chunk : 64 * chunk + 64, 0:width] = block[64:128, start : start + width]


def mix_chunks(flags, low, high, mixed, lanes):
    def step(chunk, carry):
        rows = pl.ds(pl.multiple_of(chunk * 64, 64), 64)
        chosen = flags[chunk] > 0
        mixed[rows, 0:128] = jnp.where(chosen, low[rows, lanes], jnp.zeros((64, 128), BF))
        mixed[rows, 128:256] = jnp.where(chosen, jnp.zeros((64, 128), BF), high[rows, lanes])
        return carry

    lax.fori_loop(0, 32, step, 0)


def fold_rows(value, op):
    parts = value.reshape(value.shape[0] // 8, 8, value.shape[1])
    return op(parts, axis=0)


def forward_kernel(flags, q_ref, k0, k1, k2, k3, k4, v0, v1, v2, v3, v4, att_ref, wide_ref, stat_ref,
                   k_low, k_high, v_low, v_high, k_mix, v_mix, s_one, s_two, p_one, p_two):
    fill_chunks((k0, k1, k2, k3, k4), k_low, k_high, True, 0, 320)
    fill_chunks((v0, v1, v2, v3, v4), v_low, v_high, False, 0, 320)
    stat_ref[...] = jnp.zeros(stat_ref.shape, F32)
    for index, kv_heads in HEAD_GROUPS:
        lanes = slice(128 * index, 128 * index + 128)
        n = 192 * kv_heads
        wide = 128 * ((3 * kv_heads + 1) // 2)
        columns = slice(384 * index, 384 * index + wide)
        q_all = q_ref[:, columns].astype(F32) * 0.125
        q_low = spread_heads(q_all[0:64], kv_heads).astype(BF)
        q_high = spread_heads(q_all[64:128], kv_heads).astype(BF)
        q_both = jnp.concatenate([q_low, q_high], axis=1)
        mix_chunks(flags, k_low, k_high, k_mix, lanes)
        mix_chunks(flags, v_low, v_high, v_mix, lanes)
        allowed = causal_mask(n)
        tail = jnp.where(allowed, nt(k_high[0:64, lanes], q_high), NEGATIVE)
        floor = jnp.full((8, n), NEGATIVE, F32)

        def scores(block, carry):
            max_low, max_high = carry
            rows = pl.ds(pl.multiple_of(block * 256, 256), 256)
            one = nt(k_low[rows, lanes], q_high)
            s_one[rows, 0:n] = one
            max_high = jnp.maximum(max_high, fold_rows(one, jnp.max))
            two = nt(k_mix[rows, :], q_both)
            first = jnp.where(jnp.logical_or(allowed, block > 0), two[0:64], NEGATIVE)
            two = jnp.concatenate([first, two[64:]], axis=0)
            s_two[rows, 0:n] = two
            for part in range(4):
                top = fold_rows(two[64 * part : 64 * part + 64], jnp.max)
                chosen = flags[block * 4 + part] > 0
                max_low = jnp.maximum(max_low, jnp.where(chosen, top, NEGATIVE))
                max_high = jnp.maximum(max_high, jnp.where(chosen, NEGATIVE, top))
            return max_low, max_high

        max_low, max_high = lax.fori_loop(0, 8, scores, (floor, fold_rows(tail, jnp.max)))
        max_low = jnp.max(max_low, axis=0, keepdims=True)
        max_high = jnp.max(max_high, axis=0, keepdims=True)
        tail = jnp.exp(tail - max_high)

        def weights(block, carry):
            sum_low, sum_high = carry
            rows = pl.ds(pl.multiple_of(block * 256, 256), 256)
            one = jnp.exp(s_one[rows, 0:n] - max_high)
            p_one[rows, 0:n] = one.astype(BF)
            sum_high = sum_high + fold_rows(one, jnp.sum)
            for part in range(4):
                chosen = flags[block * 4 + part] > 0
                small = pl.ds(pl.multiple_of(block * 256 + 64 * part, 64), 64)
                two = jnp.exp(s_two[small, 0:n] - jnp.where(chosen, max_low, max_high))
                p_two[small, 0:n] = two.astype(BF)
                total = fold_rows(two, jnp.sum)
                sum_low = sum_low + jnp.where(chosen, total, 0.0)
                sum_high = sum_high + jnp.where(chosen, 0.0, total)
            return sum_low, sum_high

        sum_low, sum_high = lax.fori_loop(
            0, 8, weights, (jnp.zeros((8, n), F32), fold_rows(tail, jnp.sum))
        )
        sum_low = jnp.sum(sum_low, axis=0, keepdims=True)
        sum_high = jnp.sum(sum_high, axis=0, keepdims=True)
        out_two = tn(v_mix[...], p_two[:, 0:n])
        out_high = tn(v_low[:, lanes], p_one[:, 0:n]) + out_two[128:256]
        out_high = (out_high + tn(v_high[0:64, lanes], tail.astype(BF))) / sum_high
        out_low = out_two[0:128] / sum_low
        out_low, out_high = out_low.T, out_high.T
        span = slice(384 * index, 384 * index + n)
        wide_ref[0, span, :] = out_low
        wide_ref[1, span, :] = out_high
        att_ref[0:64, columns] = unspread_heads(out_low, kv_heads).astype(BF)
        att_ref[64:128, columns] = unspread_heads(out_high, kv_heads).astype(BF)
        stat_ref[0:1, span] = max_low + jnp.log(sum_low)
        stat_ref[1:2, span] = max_high + jnp.log(sum_high)


def backward_group(group, flags, q_ref, d_ref, wide_ref, stat_ref, k_pieces, v_pieces, dq_ref, dk_all, dv_all,
                   k_low, k_high, v_low, v_high, k_mix, v_mix):
    fill_chunks(k_pieces, k_low, k_high, True, 128 * group, 128 if group < 2 else 64)
    fill_chunks(v_pieces, v_low, v_high, False, 128 * group, 128 if group < 2 else 64)
    for index, kv_heads in HEAD_GROUPS[group : group + 1]:
        lanes = slice(0, 128)
        n = 192 * kv_heads
        wide = 128 * ((3 * kv_heads + 1) // 2)
        columns = slice(384 * index, 384 * index + wide)
        span = slice(384 * index, 384 * index + n)
        q_all = q_ref[:, columns].astype(F32) * 0.125
        d_all = d_ref[:, columns].astype(F32)
        q_low = spread_heads(q_all[0:64], kv_heads).astype(BF)
        q_high = spread_heads(q_all[64:128], kv_heads).astype(BF)
        q_both = jnp.concatenate([q_low, q_high], axis=1)
        d_low = spread_heads(d_all[0:64], kv_heads)
        d_high = spread_heads(d_all[64:128], kv_heads)
        ones = jnp.ones((8, 128), F32)

        def row_sums(value):
            return lax.dot_general(
                ones, value, (((1,), (1,)), ((), ())),
                precision=lax.Precision.HIGHEST, preferred_element_type=F32,
            )[0:1]

        delta_low = row_sums(d_low * wide_ref[0, span, :])
        delta_high = row_sums(d_high * wide_ref[1, span, :])
        d_low, d_high = d_low.astype(BF), d_high.astype(BF)
        d_both = jnp.concatenate([d_low, d_high], axis=1)
        log_low, log_high = stat_ref[0:1, span], stat_ref[1:2, span]
        mix_chunks(flags, k_low, k_high, k_mix, lanes)
        mix_chunks(flags, v_low, v_high, v_mix, lanes)
        allowed = causal_mask(n)

        own_k, own_v = k_high[0:64, lanes], v_high[0:64, lanes]
        soft = jnp.where(allowed, jnp.exp(nt(own_k, q_high) - log_high), 0.0)
        grad = (soft * (nt(own_v, d_high) - delta_high)).astype(BF)
        tail_k = matrix_product(grad, q_high)
        tail_v = matrix_product(soft.astype(BF), d_high)
        start_high = tn(own_k, grad)

        def step(block, carry):
            dq_low, dq_high = carry
            rows = pl.ds(pl.multiple_of(block * 256, 256), 256)
            k_one, v_one = k_low[rows, lanes], v_low[rows, lanes]
            soft = jnp.exp(nt(k_one, q_high) - log_high)
            grad = (soft * (nt(v_one, d_high) - delta_high)).astype(BF)
            dk_one = matrix_product(grad, q_high)
            dv_one = matrix_product(soft.astype(BF), d_high)
            dq_high = dq_high + tn(k_one, grad)
            k_two, v_two = k_mix[rows, :], v_mix[rows, :]
            two = nt(k_two, q_both)
            two_grad = nt(v_two, d_both)
            softs, grads = [], []
            for part in range(4):
                chosen = flags[block * 4 + part] > 0
                inner = slice(64 * part, 64 * part + 64)
                soft = jnp.exp(two[inner] - jnp.where(chosen, log_low, log_high))
                if part == 0:
                    soft = jnp.where(jnp.logical_or(allowed, block > 0), soft, 0.0)
                softs.append(soft.astype(BF))
                grads.append(
                    (soft * (two_grad[inner] - jnp.where(chosen, delta_low, delta_high))).astype(BF)
                )
            soft = jnp.concatenate(softs, axis=0)
            grad = jnp.concatenate(grads, axis=0)
            dk_two = matrix_product(grad, q_both)
            dv_two = matrix_product(soft, d_both)
            both = tn(k_two, grad)
            for part in range(4):
                chosen = flags[block * 4 + part] > 0
                inner = slice(64 * part, 64 * part + 64)
                chunk = block * 4 + part
                for one, other, out in ((dk_one, dk_two, dk_all), (dv_one, dv_two, dv_all)):
                    out[chunk, 0:64, lanes] = (
                        one[inner] + jnp.where(chosen, other[inner, 0:128], 0.0)
                    ).astype(BF)
                    out[chunk, 64:128, lanes] = jnp.where(chosen, 0.0, other[inner, 128:256]).astype(BF)
            return dq_low + both[0:128], dq_high + both[128:256]

        dq_low, dq_high = lax.fori_loop(0, 8, step, (jnp.zeros((128, n), F32), start_high))
        dk_all[0, 64:128, lanes] = tail_k.astype(BF)
        dv_all[0, 64:128, lanes] = tail_v.astype(BF)
        dq_ref[0:64, :] = unspread_heads(dq_low.T, kv_heads) * 0.125
        dq_ref[64:128, :] = unspread_heads(dq_high.T, kv_heads) * 0.125


def backward_part(group, flags, q_ref, d_ref, wide_ref, stat_ref, k0, k1, k2, k3, k4, v0, v1, v2, v3, v4,
                  dq_ref, dk_ref, dv_ref, *scratch):
    backward_group(group, flags, q_ref, d_ref, wide_ref, stat_ref, (k0, k1, k2, k3, k4), (v0, v1, v2, v3, v4),
                   dq_ref, dk_ref, dv_ref, *scratch)


def backward_last(group, flags, q_ref, d_ref, wide_ref, stat_ref, k0, k1, k2, k3, k4, v0, v1, v2, v3, v4,
                  dk_a, dk_b, dv_a, dv_b,
                  dq_ref, dk0, dk1, dk2, dk3, dk4, dv0, dv1, dv2, dv3, dv4, dk_c, dv_c, *scratch):
    backward_group(group, flags, q_ref, d_ref, wide_ref, stat_ref, (k0, k1, k2, k3, k4), (v0, v1, v2, v3, v4),
                   dq_ref, dk_c, dv_c, *scratch)
    for pieces, wholes, outer_first in (
        ((dk0, dk1, dk2, dk3, dk4), (dk_a, dk_b, dk_c), True),
        ((dv0, dv1, dv2, dv3, dv4), (dv_a, dv_b, dv_c), False),
    ):
        for chunk in range(32):
            one, two, zed = chunk // 8, (chunk // 2) % 4, chunk % 2
            outer, inner = (one, two) if outer_first else (two, one)
            if outer < 3:
                piece, place = pieces[outer], 2 * inner + zed
            else:
                piece, place = pieces[3 + inner // 2], 2 * (inner % 2) + zed
            piece[place, :, 0:128] = wholes[0][chunk]
            piece[place, :, 128:256] = wholes[1][chunk]
            piece[place, :, 256:320] = wholes[2][chunk, :, 0:64]


VMEM_SPEC = pl.BlockSpec(memory_space=pltpu.VMEM)
SMEM_SPEC = pl.BlockSpec(memory_space=pltpu.SMEM)
LIMIT = pltpu.CompilerParams(vmem_limit_bytes=50 * 1024 * 1024)


def kv_scratch(lanes):
    return [pltpu.VMEM((2048, lanes), BF) for _ in range(4)] + [pltpu.VMEM((2048, 256), BF) for _ in range(2)]


def cost(products):
    return pl.CostEstimate(
        flops=products * 2 * 128 * 4096 * 64, bytes_accessed=6_000_000, transcendentals=128 * 2048 * 6
    )


def attention_forward(flags, queries, keys, values):
    return pl.pallas_call(
        forward_kernel,
        out_shape=(
            jax.ShapeDtypeStruct((128, 1024), BF),
            jax.ShapeDtypeStruct((2, 960, 128), F32),
            jax.ShapeDtypeStruct((8, 1024), F32),
        ),
        in_specs=[SMEM_SPEC] + [VMEM_SPEC] * 11,
        out_specs=(VMEM_SPEC,) * 3,
        scratch_shapes=kv_scratch(384)
        + [pltpu.VMEM((2048, 384), F32) for _ in range(2)]
        + [pltpu.VMEM((2048, 384), BF) for _ in range(2)],
        compiler_params=LIMIT,
        cost_estimate=cost(60),
        name="attention_forward",
    )(flags, queries, *keys, *values)


def attention_backward(group, flags, queries, gradient, wide, stats, keys, values, earlier=()):
    whole = [jax.ShapeDtypeStruct((32, 128, 128), BF)] * 2
    pieces = [jax.ShapeDtypeStruct((count, 128, 320), BF) for count in (8, 8, 8, 4, 4)] * 2
    scratch = kv_scratch(128)
    if earlier:
        scratch = [pltpu.VMEM((32, 128, 128), BF) for _ in range(2)] + scratch
    outs = [jax.ShapeDtypeStruct((128, 384 if group < 2 else 256), F32)] + (pieces if earlier else whole)
    return pl.pallas_call(
        functools.partial(backward_last if earlier else backward_part, group),
        out_shape=tuple(outs),
        in_specs=[SMEM_SPEC] + [VMEM_SPEC] * (14 + len(earlier)),
        out_specs=(VMEM_SPEC,) * len(outs),
        scratch_shapes=scratch,
        compiler_params=LIMIT,
        cost_estimate=cost(40),
        name="attention_backward",
    )(flags, queries, gradient, wide, stats, *keys, *values, *earlier)


def body(
    tokens, block_pairs, w_query, key_weight, value_weight, w_out, gain_attn, gain_mlp, w_gate, w_up, w_down, cotangent
):
    rows, width = tokens.shape[1:]
    kv_width = KEY_VALUE_HEADS * HEAD_SIZE
    x_here, y_here, z_here = lax.axis_index("x"), lax.axis_index("y"), lax.axis_index("zh")
    place = 2 * lax.axis_index("zl") + lax.axis_index("co")
    context = z_here * 16 + x_here * 4 + y_here

    weights_in = weight_gather(jnp.concatenate([w_query, key_weight, value_weight], axis=1))
    gains = lax.all_gather(jnp.stack([gain_attn, gain_mlp])[None], FS, axis=0, tiled=True)
    gains = jnp.swapaxes(gains, 0, 1).reshape(2, width).astype(F32)
    gain_one, gain_two = gains[0], gains[1]

    inputs = tokens[0].astype(F32)
    upstream = cotangent[0].astype(F32)
    order = [
        ((z_here + z) % 2) * 16 + ((x_here + x + 4) % 4) * 4 + (y_here + y + 4) % 4
        for x in RING
        for y in RING
        for z in (0, 1)
    ]
    pairs = block_pairs[0][jnp.stack(order)]
    flags = jnp.where(jnp.arange(32) == 0, 1, (pairs < pairs[0]).astype(jnp.int32))
    offsets = jnp.arange(rows // 2, dtype=jnp.int32)
    query_places = jnp.concatenate(
        [pairs[0] * (rows // 2) + offsets, (63 - pairs[0]) * (rows // 2) + offsets]
    )
    frequency = 10000.0 ** (-jnp.arange(HEAD_SIZE // 2, dtype=F32) / (HEAD_SIZE // 2))
    angles = query_places.astype(F32)[:, None] * frequency[None, :]
    cosine_table, sinusoid_table = jnp.cos(angles)[:, None, :], jnp.sin(angles)[:, None, :]

    normed_one, inverse_one = norm_forward(inputs, gain_one)
    normed_low = normed_one.astype(BF)
    projected = matrix_product(normed_low, weights_in)
    heads = QUERY_HEADS + KEY_VALUE_HEADS
    rotated = apply_rotation(
        projected[:, : width + kv_width].reshape(rows, heads, HEAD_SIZE), cosine_table, sinusoid_table
    ).astype(BF)
    queries = rotated[:, :QUERY_HEADS]
    keys = rotated[:, QUERY_HEADS:].reshape(rows, kv_width)
    values = projected[:, width + kv_width :].astype(BF)

    all_keys, all_values = context_gather(keys, values)
    late_out, late_cotangent, _ = together(w_out, cotangent[0], all_keys[0])
    out_w = weight_gather(late_out)
    grad_mlp = pair_gather(late_cotangent).reshape(4 * rows, width)
    lane_pad = ((0, 0), (0, 64))
    flat_queries = jnp.pad(queries.reshape(rows, width), lane_pad)
    attended_low, attended_wide, stats = attention_forward(flags, flat_queries, all_keys, all_values)
    attended_low = attended_low[:, :width]
    middle = inputs + matrix_product(attended_low, out_w)
    normed_two, inverse_two = norm_forward(middle, gain_two)
    normed_mlp = pair_gather(normed_two.astype(BF)).reshape(4 * rows, width)

    gate_pre = matrix_product(normed_mlp, w_gate)
    up_pre = matrix_product(normed_mlp, w_up)
    grad_hidden = right_inner(grad_mlp, w_down)
    sigmoid_gate = jax.nn.sigmoid(gate_pre)
    hidden = (gate_pre * sigmoid_gate * up_pre).astype(BF)
    grad_up_pre = (grad_hidden * gate_pre * sigmoid_gate).astype(BF)
    grad_gate_pre = (
        grad_hidden * up_pre * sigmoid_gate * (1.0 + gate_pre * (1.0 - sigmoid_gate))
    ).astype(BF)
    grad_normed_two = right_inner(grad_gate_pre, w_gate) + right_inner(grad_up_pre, w_up)
    grad_normed_two = pair_scatter(grad_normed_two.astype(BF).reshape(4, rows, width))
    mlp_term = pair_scatter(matrix_product(hidden, w_down).astype(BF).reshape(4, rows, width))
    result = (middle + mlp_term).astype(BF)[None]

    pad = ((0, 64), (0, 0))
    grad_gate_w = jnp.pad(left_inner(normed_mlp, grad_gate_pre).astype(BF), pad).reshape(16, 64, -1)
    grad_up_w = jnp.pad(left_inner(normed_mlp, grad_up_pre).astype(BF), pad).reshape(16, 64, -1)
    grad_down_w = jnp.pad(left_inner(grad_mlp, hidden).astype(BF), pad).reshape(2, 16, 32, -1)
    pack_one = jnp.concatenate([grad_gate_w, grad_down_w[0]], axis=1)
    pack_two = jnp.concatenate([grad_up_w, grad_down_w[1]], axis=1)
    hidden_shard = w_gate.shape[1]
    pieces = []
    for pack, axis in ((pack_one, "x"), (pack_two, "y")):
        own, left, right, far = ring_pick(pack.reshape(4, 4, 96, hidden_shard), axis)
        pieces.append((own, left, right, far[:2], far[2:]))

    through_two, grad_gain_two = norm_backward(middle, inverse_two, gain_two, grad_normed_two)
    grad_middle = upstream + through_two
    grad_branch = grad_middle.astype(BF)
    attended_gradient = right_inner(grad_branch, out_w).astype(BF)
    back = (
        flat_queries,
        jnp.pad(attended_gradient, lane_pad),
        attended_wide,
        stats,
        all_keys,
        all_values,
    )
    far = ring_far(*pieces, "x", "y")
    dq_a, dk_a, dv_a = attention_backward(0, flags, *back)
    flags_b, far, _ = together(flags, far, dq_a)
    sums = ring_near(*pieces, far, "x", "y")
    dq_b, dk_b, dv_b = attention_backward(1, flags_b, *back)
    flags_c, sum_one, sum_two, _ = together(flags_b, *sums, dq_b)
    near = near_scatter(ring_pick(sum_one, "y"), "y") + near_scatter(ring_pick(sum_two, "x"), "x")
    last_part = attention_backward(2, flags_c, *back, earlier=(dk_a, dk_b, dv_a, dv_b))
    near = together(last_part[0], *near)
    dq_c, near = near[0], near[1:]
    pack_slot = jnp.concatenate([add_low(*near[:4]), add_low(*near[4:])], axis=0)
    grad_queries = jnp.concatenate([dq_a, dq_b, dq_c], axis=1)
    own_key_gradient, own_value_gradient = context_scatter(last_part[1:6], last_part[6:11])
    pack_slot = add_low(pack_slot, shift(pack_slot, "zh", 1))
    pack_all = lax.all_gather(pack_slot[None], ("x", "y"), axis=0, tiled=True)
    grad_query_pre = (
        apply_rotation(grad_queries[:, :width].reshape(rows, QUERY_HEADS, HEAD_SIZE), cosine_table, -sinusoid_table)
        .reshape(rows, width)
        .astype(BF)
    )
    grad_key_pre = (
        apply_rotation(
            own_key_gradient.reshape(rows, KEY_VALUE_HEADS, HEAD_SIZE), cosine_table, -sinusoid_table
        )
        .reshape(rows, kv_width)
        .astype(BF)
    )
    grad_kv = jnp.concatenate([grad_key_pre, own_value_gradient.astype(BF)], axis=1)

    quarter = width // 4
    columns = jnp.stack([normed_low.T.reshape(4, quarter, rows), attended_low.T.reshape(4, quarter, rows)], axis=1)
    columns = column_exchange(columns, place)
    early = pair_gather(jnp.concatenate([grad_branch, grad_query_pre], axis=1)).reshape(4 * rows, 2 * width)
    grad_out_w = matrix_product(columns[1], early[:, :width]).astype(BF)
    grad_query_w = matrix_product(columns[0], early[:, width:]).astype(BF)
    all_kv = pair_gather(grad_kv).reshape(4 * rows, 2 * kv_width)
    grad_kv_w = matrix_product(columns[0], all_kv).astype(BF)
    grad_normed_one = right_inner(jnp.concatenate([grad_query_pre, grad_kv], axis=1), weights_in)
    through_one, grad_gain_one = norm_backward(inputs, inverse_one, gain_one, grad_normed_one)
    input_grad = (grad_middle + through_one)[None]

    grad_gains = jnp.stack([grad_gain_one, grad_gain_two]).reshape(2, 4, 1, quarter)
    gain_parts = [
        lax.dynamic_index_in_dim(grad_gains, place ^ mask, axis=1, keepdims=False) for mask in range(4)
    ]
    near_gains = jnp.stack(gain_parts[:2]) + shift(jnp.stack(gain_parts[2:]), "zl", 1)
    gains_row = (near_gains[0] + shift(near_gains[1], "co", 1)).reshape(1, 2 * quarter).astype(BF)
    last = jnp.concatenate([grad_out_w, grad_query_w, grad_kv_w], axis=1)
    last = jnp.concatenate([last, jnp.pad(gains_row, ((0, 15), (0, last.shape[1] - 2 * quarter)))], axis=0)
    out = add_low(*together(*near_scatter(ring_pick(last.reshape(4, 4, 16, -1), "x"), "x")))
    out = add_low(*together(*near_scatter(ring_pick(out, "y"), "y")))
    out = add_low(out, shift(out, "zh", 1))
    out = ring_place(near_gather(out, "y"), "y")
    sum_last = ring_place(near_gather(out, "x"), "x").reshape(256, -1)

    one = pack_all[:, :96]
    two = jnp.swapaxes(pack_all[:, 96:].reshape(4, 4, 96, hidden_shard), 0, 1).reshape(16, 96, hidden_shard)
    sum_down = jnp.concatenate(
        [one[:, 64:].reshape(512, hidden_shard), two[:, 64:].reshape(512, hidden_shard)], axis=0
    )[:width]
    return (
        result,
        input_grad,
        sum_last[:quarter, width : 2 * width].astype(F32),
        sum_last[:quarter, 2 * width : 2 * width + kv_width].astype(F32),
        sum_last[:quarter, 2 * width + kv_width :].astype(F32),
        sum_last[:quarter, :width].astype(F32),
        sum_last[quarter, :quarter].astype(F32),
        sum_last[quarter, quarter : 2 * quarter].astype(F32),
        one[:, :64].reshape(1024, hidden_shard)[:width].astype(F32),
        two[:, :64].reshape(1024, hidden_shard)[:width].astype(F32),
        sum_down.T.astype(F32),
    )


def solution(mesh):
    split = Mesh(mesh.devices.reshape(2, 4, 4, 2, 2), ("zh", "x", "y", "zl", "co"))
    ctx = ("zh", "x", "y")
    in_specs = (
        P(FS, ctx, None),
        P(FS, None),
        P(FS, None),
        P(FS, None),
        P(FS, None),
        P(FS, None),
        P(FS),
        P(FS),
        P(None, FS),
        P(None, FS),
        P(FS, None),
        P(FS, ctx, None),
    )
    out_specs = (
        P(FS, ctx, None),
        P(FS, ctx, None),
        P(FS, None),
        P(FS, None),
        P(FS, None),
        P(FS, None),
        P(FS),
        P(FS),
        P(None, FS),
        P(None, FS),
        P(FS, None),
    )
    return jax.shard_map(body, mesh=split, in_specs=in_specs, out_specs=out_specs, check_vma=False)
```

```python
import functools

import jax
import jax.numpy as jnp
from jax import lax
from jax.experimental import pallas as pl
from jax.experimental.pallas import tpu as pltpu
from jax.sharding import Mesh, PartitionSpec as P

QUERY_HEADS = 15
KEY_VALUE_HEADS = 5
HEAD_SIZE = 64
EPSILON = 1e-05
BF = jnp.bfloat16
F32 = jnp.float32
FS = ("zl", "co")
RING = (0, -1, 1, 2)


def matrix_product(left, right):
    return jnp.dot(left, right, preferred_element_type=F32)


def left_inner(left, right):
    return lax.dot_general(left, right, (((0,), (0,)), ((), ())), preferred_element_type=F32)


def right_inner(left, right):
    return lax.dot_general(left, right, (((1,), (1,)), ((), ())), preferred_element_type=F32)


def shift(value, axis, step):
    count = lax.axis_size(axis)
    return lax.ppermute(value, axis, [(i, (i + step) % count) for i in range(count)])


def add_low(*parts):
    total = parts[0].astype(F32)
    for part in parts[1:]:
        total = total + part.astype(F32)
    return total.astype(BF)


def together(*values):
    return lax.optimization_barrier(values)


def ring_pick(value, axis):
    here = lax.axis_index(axis)
    return [
        lax.dynamic_index_in_dim(value, lax.rem(here + off + 4, 4), axis=0, keepdims=False) for off in RING
    ]


def ring_place(blocks, axis):
    here = lax.axis_index(axis)
    out = jnp.stack(blocks)
    for block, off in zip(blocks, RING):
        out = lax.dynamic_update_slice_in_dim(out, block[None], lax.rem(here + off + 4, 4), axis=0)
    return out


def near_gather(value, axis):
    return [value, shift(value, axis, 1), shift(value, axis, -1), shift(value, axis, 2)]


def near_scatter(blocks, axis):
    return [blocks[0], shift(blocks[1], axis, -1), shift(blocks[2], axis, 1), shift(blocks[3], axis, 2)]


def two_ring_gather(one, two, axis_one, axis_two):
    left_one, right_one, left_two, right_two = (
        shift(one, axis_one, 1), shift(one, axis_one, -1), shift(two, axis_two, 1), shift(two, axis_two, -1)
    )
    half = one.shape[0] // 2
    far = (
        shift(left_one[:half], axis_one, 1),
        shift(right_one[half:], axis_one, -1),
        shift(left_two[:half], axis_two, 1),
        shift(right_two[half:], axis_two, -1),
    )
    return (one, left_one, right_one, far[0], far[1]), (two, left_two, right_two, far[2], far[3])


def ring_far(one, two, axis_one, axis_two):
    return (
        shift(one[3], axis_one, 1), shift(one[4], axis_one, -1), shift(two[3], axis_two, 1), shift(two[4], axis_two, -1)
    )


def pair_gather(value):
    both = jnp.concatenate([value[None], shift(value, "zl", 1)[None]], axis=0)
    other = shift(both, "co", 1)
    return jnp.stack([both[0], other[0], both[1], other[1]])


def pair_blocks(value):
    far = shift(value, "zl", 1)
    return value, shift(value, "co", 1), far, shift(far, "co", 1)


def pair_scatter(value):
    near = add_low(value[:2], shift(value[2:].astype(BF), "zl", 1))
    return near[0].astype(F32) + shift(near[1], "co", 1).astype(F32)


def weight_blocks(value):
    cut = 128
    zed = ("zh", "zl")
    one = shift(value[:cut], zed, 1)
    two = shift(value[cut:], zed, -1)
    return value, shift(value, "co", 1), one, two, shift(one, "co", 1), shift(two, "co", 1)


def context_gather(both):
    width = both.shape[1] // 2
    both = jnp.stack([both, shift(both, "zh", 1)])
    keys = jnp.concatenate(near_gather(both[:, :, :width], "y"))
    values = jnp.concatenate(near_gather(both[:, :, width:], "x"))
    return two_ring_gather(keys, values, "x", "y")


def slot_sum(value, axes):
    parts = lax.all_to_all(value, axes, 0, 0, tiled=True)
    return jnp.sum(parts.astype(F32), axis=0)


def slot_gather(value, axes):
    count = lax.axis_size(axes)
    return lax.all_to_all(jnp.broadcast_to(value[None], (count,) + value.shape), axes, 0, 0, tiled=True)


def column_exchange(value, place):
    mine = lax.dynamic_index_in_dim(value, place, axis=0, keepdims=False)
    parts = [mine] + [
        lax.dynamic_index_in_dim(value, place ^ mask, axis=0, keepdims=False) for mask in (1, 2, 3)
    ]
    from_z = shift(jnp.stack(parts[2:]), "zl", 1)
    from_core = shift(jnp.stack([parts[1], from_z[1]]), "co", 1)
    return jnp.concatenate([mine, from_core[0], from_z[0], from_core[1]], axis=-1)


def apply_rotation(values, cosine_table, sinusoid_table):
    half = values.shape[-1] // 2
    leading, trailing = values[..., :half], values[..., half:]
    return jnp.concatenate(
        [
            leading * cosine_table - trailing * sinusoid_table,
            trailing * cosine_table + leading * sinusoid_table,
        ],
        axis=-1,
    )


def norm_forward(values, gain_vector):
    inverse = lax.rsqrt(jnp.mean(values * values, axis=-1, keepdims=True) + EPSILON)
    return (values * inverse * gain_vector, inverse)


def norm_backward(values, inverse, gain_vector, gradient):
    weighted = gradient * gain_vector
    through = inverse * weighted - values * inverse**3 * jnp.mean(
        weighted * values, axis=-1, keepdims=True
    )
    return (through, jnp.sum(gradient * values * inverse, axis=0))


HEAD_GROUPS = ((0, 2), (1, 2), (2, 1))
NEGATIVE = -1e30


def nt(left, right):
    return lax.dot_general(left, right, (((1,), (1,)), ((), ())), preferred_element_type=F32)


def tn(left, right):
    return lax.dot_general(left, right, (((0,), (0,)), ((), ())), preferred_element_type=F32)


def swap_halves(slab):
    return jnp.concatenate([slab[:, 64:], slab[:, :64]], axis=1)


def spread_heads(rows, kv_heads):
    lane = lax.broadcasted_iota(jnp.int32, (64, 128), 1)
    blocks = []
    for kv in range(kv_heads):
        for group in range(3):
            head = 3 * kv + group
            slab = rows[:, 128 * (head // 2) : 128 * (head // 2) + 128]
            if head % 2 != kv:
                slab = swap_halves(slab)
            blocks.append(jnp.where((lane < 64) == (kv == 0), slab, 0.0))
    return jnp.concatenate(blocks, axis=0)


def unspread_heads(blocks, kv_heads):
    lane = lax.broadcasted_iota(jnp.int32, (64, 128), 1)
    count = 3 * kv_heads
    slabs = []
    for slab in range((count + 1) // 2):
        halves = []
        for side in range(2):
            head = 2 * slab + side
            if head >= count:
                halves.append(jnp.zeros((64, 128), F32))
                continue
            block = blocks[64 * head : 64 * head + 64]
            halves.append(block if head // 3 == side else swap_halves(block))
        slabs.append(jnp.where(lane < 64, halves[0], halves[1]))
    return jnp.concatenate(slabs, axis=1)


def causal_mask(columns):
    key = lax.broadcasted_iota(jnp.int32, (64, columns), 0)
    query = lax.rem(lax.broadcasted_iota(jnp.int32, (64, columns), 1), 64)
    return key <= query


def fill_chunks(pieces, low, high, outer_first, start, width):
    if width % 128:
        zeros = jnp.zeros((2048, 64), BF)
        low[:, width : width + 64] = zeros
        high[:, width : width + 64] = zeros
    for chunk in range(32):
        one, two, zed = chunk // 8, (chunk // 2) % 4, chunk % 2
        outer, inner = (one, two) if outer_first else (two, one)
        if outer < 3:
            block = pieces[outer].at[2 * inner + zed]
        else:
            block = pieces[3 + inner // 2].at[2 * (inner % 2) + zed]
        low[64 * chunk : 64 * chunk + 64, 0:width] = block[0:64, start : start + width]
        high[64 * chunk : 64 * chunk + 64, 0:width] = block[64:128, start : start + width]


def mix_chunks(flags, low, high, mixed, lanes):
    def step(chunk, carry):
        rows = pl.ds(pl.multiple_of(chunk * 64, 64), 64)
        chosen = flags[chunk] > 0
        mixed[rows, 0:128] = jnp.where(chosen, low[rows, lanes], jnp.zeros((64, 128), BF))
        mixed[rows, 128:256] = jnp.where(chosen, jnp.zeros((64, 128), BF), high[rows, lanes])
        return carry

    lax.fori_loop(0, 32, step, 0)


def fold_rows(value, op):
    parts = value.reshape(value.shape[0] // 8, 8, value.shape[1])
    return op(parts, axis=0)


def forward_kernel(flags, q_ref, k0, k1, k2, k3, k4, v0, v1, v2, v3, v4, att_ref, wide_ref, stat_ref,
                   k_low, k_high, v_low, v_high, k_mix, v_mix, s_one, s_two, p_one, p_two):
    fill_chunks((k0, k1, k2, k3, k4), k_low, k_high, True, 0, 320)
    fill_chunks((v0, v1, v2, v3, v4), v_low, v_high, False, 0, 320)
    stat_ref[...] = jnp.zeros(stat_ref.shape, F32)
    for index, kv_heads in HEAD_GROUPS:
        lanes = slice(128 * index, 128 * index + 128)
        n = 192 * kv_heads
        wide = 128 * ((3 * kv_heads + 1) // 2)
        columns = slice(384 * index, 384 * index + wide)
        q_all = q_ref[:, columns].astype(F32) * 0.125
        q_low = spread_heads(q_all[0:64], kv_heads).astype(BF)
        q_high = spread_heads(q_all[64:128], kv_heads).astype(BF)
        q_both = jnp.concatenate([q_low, q_high], axis=1)
        mix_chunks(flags, k_low, k_high, k_mix, lanes)
        mix_chunks(flags, v_low, v_high, v_mix, lanes)
        allowed = causal_mask(n)
        tail = jnp.where(allowed, nt(k_high[0:64, lanes], q_high), NEGATIVE)
        floor = jnp.full((8, n), NEGATIVE, F32)

        def scores(block, carry):
            max_low, max_high = carry
            rows = pl.ds(pl.multiple_of(block * 256, 256), 256)
            one = nt(k_low[rows, lanes], q_high)
            s_one[rows, 0:n] = one
            max_high = jnp.maximum(max_high, fold_rows(one, jnp.max))
            two = nt(k_mix[rows, :], q_both)
            first = jnp.where(jnp.logical_or(allowed, block > 0), two[0:64], NEGATIVE)
            two = jnp.concatenate([first, two[64:]], axis=0)
            s_two[rows, 0:n] = two
            for part in range(4):
                top = fold_rows(two[64 * part : 64 * part + 64], jnp.max)
                chosen = flags[block * 4 + part] > 0
                max_low = jnp.maximum(max_low, jnp.where(chosen, top, NEGATIVE))
                max_high = jnp.maximum(max_high, jnp.where(chosen, NEGATIVE, top))
            return max_low, max_high

        max_low, max_high = lax.fori_loop(0, 8, scores, (floor, fold_rows(tail, jnp.max)))
        max_low = jnp.max(max_low, axis=0, keepdims=True)
        max_high = jnp.max(max_high, axis=0, keepdims=True)
        tail = jnp.exp(tail - max_high)

        def weights(block, carry):
            sum_low, sum_high = carry
            rows = pl.ds(pl.multiple_of(block * 256, 256), 256)
            one = jnp.exp(s_one[rows, 0:n] - max_high)
            p_one[rows, 0:n] = one.astype(BF)
            sum_high = sum_high + fold_rows(one, jnp.sum)
            for part in range(4):
                chosen = flags[block * 4 + part] > 0
                small = pl.ds(pl.multiple_of(block * 256 + 64 * part, 64), 64)
                two = jnp.exp(s_two[small, 0:n] - jnp.where(chosen, max_low, max_high))
                p_two[small, 0:n] = two.astype(BF)
                total = fold_rows(two, jnp.sum)
                sum_low = sum_low + jnp.where(chosen, total, 0.0)
                sum_high = sum_high + jnp.where(chosen, 0.0, total)
            return sum_low, sum_high

        sum_low, sum_high = lax.fori_loop(
            0, 8, weights, (jnp.zeros((8, n), F32), fold_rows(tail, jnp.sum))
        )
        sum_low = jnp.sum(sum_low, axis=0, keepdims=True)
        sum_high = jnp.sum(sum_high, axis=0, keepdims=True)
        out_two = tn(v_mix[...], p_two[:, 0:n])
        out_high = tn(v_low[:, lanes], p_one[:, 0:n]) + out_two[128:256]
        out_high = (out_high + tn(v_high[0:64, lanes], tail.astype(BF))) / sum_high
        out_low = out_two[0:128] / sum_low
        out_low, out_high = out_low.T, out_high.T
        span = slice(384 * index, 384 * index + n)
        wide_ref[0, span, :] = out_low
        wide_ref[1, span, :] = out_high
        att_ref[0:64, columns] = unspread_heads(out_low, kv_heads).astype(BF)
        att_ref[64:128, columns] = unspread_heads(out_high, kv_heads).astype(BF)
        stat_ref[0:1, span] = max_low + jnp.log(sum_low)
        stat_ref[1:2, span] = max_high + jnp.log(sum_high)


def rotate_slabs(value, cosine, sine):
    lane = lax.broadcasted_iota(jnp.int32, (value.shape[0], 128), 1)
    slabs = []
    for start in range(0, value.shape[1], 128):
        slab = value[:, start : start + 128]
        other = jnp.where(lane % 64 < 32, pltpu.roll(slab, 96, 1), pltpu.roll(slab, 32, 1))
        slabs.append(slab * cosine + other * sine)
    return jnp.concatenate(slabs, axis=1)


def backward_kernel(flags, q_ref, d_ref, wide_ref, stat_ref, cos_ref, sin_ref,
                    k0, k1, k2, k3, k4, v0, v1, v2, v3, v4,
                    dq_ref, dk0, dk1, dk2, dk3, dk4, dv0, dv1, dv2, dv3, dv4,
                    k_low, k_high, v_low, v_high, k_mix, v_mix, dk_all, dv_all):
    for index, kv_heads in HEAD_GROUPS:
        fill_chunks((k0, k1, k2, k3, k4), k_low, k_high, True, 128 * index, 64 * kv_heads)
        fill_chunks((v0, v1, v2, v3, v4), v_low, v_high, False, 128 * index, 64 * kv_heads)
        lanes = slice(0, 128)
        n = 192 * kv_heads
        wide = 128 * ((3 * kv_heads + 1) // 2)
        columns = slice(384 * index, 384 * index + wide)
        span = slice(384 * index, 384 * index + n)
        q_all = q_ref[:, columns].astype(F32) * 0.125
        d_all = d_ref[:, columns].astype(F32)
        q_low = spread_heads(q_all[0:64], kv_heads).astype(BF)
        q_high = spread_heads(q_all[64:128], kv_heads).astype(BF)
        q_both = jnp.concatenate([q_low, q_high], axis=1)
        d_low = spread_heads(d_all[0:64], kv_heads)
        d_high = spread_heads(d_all[64:128], kv_heads)
        ones = jnp.ones((8, 128), F32)

        def row_sums(value):
            return lax.dot_general(
                ones, value, (((1,), (1,)), ((), ())),
                precision=lax.Precision.HIGHEST, preferred_element_type=F32,
            )[0:1]

        delta_low = row_sums(d_low * wide_ref[0, span, :])
        delta_high = row_sums(d_high * wide_ref[1, span, :])
        d_low, d_high = d_low.astype(BF), d_high.astype(BF)
        d_both = jnp.concatenate([d_low, d_high], axis=1)
        log_low, log_high = stat_ref[0:1, span], stat_ref[1:2, span]
        mix_chunks(flags, k_low, k_high, k_mix, lanes)
        mix_chunks(flags, v_low, v_high, v_mix, lanes)
        allowed = causal_mask(n)

        own_k, own_v = k_high[0:64, lanes], v_high[0:64, lanes]
        soft = jnp.where(allowed, jnp.exp(nt(own_k, q_high) - log_high), 0.0)
        grad = (soft * (nt(own_v, d_high) - delta_high)).astype(BF)
        tail_k = matrix_product(grad, q_high)
        tail_v = matrix_product(soft.astype(BF), d_high)
        start_high = tn(own_k, grad)

        def step(block, carry):
            dq_low, dq_high = carry
            rows = pl.ds(pl.multiple_of(block * 256, 256), 256)
            k_one, v_one = k_low[rows, lanes], v_low[rows, lanes]
            soft = jnp.exp(nt(k_one, q_high) - log_high)
            grad = (soft * (nt(v_one, d_high) - delta_high)).astype(BF)
            dk_one = matrix_product(grad, q_high)
            dv_one = matrix_product(soft.astype(BF), d_high)
            dq_high = dq_high + tn(k_one, grad)
            k_two, v_two = k_mix[rows, :], v_mix[rows, :]
            two = nt(k_two, q_both)
            two_grad = nt(v_two, d_both)
            softs, grads = [], []
            for part in range(4):
                chosen = flags[block * 4 + part] > 0
                inner = slice(64 * part, 64 * part + 64)
                soft = jnp.exp(two[inner] - jnp.where(chosen, log_low, log_high))
                if part == 0:
                    soft = jnp.where(jnp.logical_or(allowed, block > 0), soft, 0.0)
                softs.append(soft.astype(BF))
                grads.append(
                    (soft * (two_grad[inner] - jnp.where(chosen, delta_low, delta_high))).astype(BF)
                )
            soft = jnp.concatenate(softs, axis=0)
            grad = jnp.concatenate(grads, axis=0)
            dk_two = matrix_product(grad, q_both)
            dv_two = matrix_product(soft, d_both)
            both = tn(k_two, grad)
            for part in range(4):
                chosen = flags[block * 4 + part] > 0
                inner = slice(64 * part, 64 * part + 64)
                chunk = block * 4 + part
                for one, other, out in ((dk_one, dk_two, dk_all), (dv_one, dv_two, dv_all)):
                    out[chunk, 0:64, :] = (one[inner] + jnp.where(chosen, other[inner, 0:128], 0.0)).astype(BF)
                    out[chunk, 64:128, :] = jnp.where(chosen, 0.0, other[inner, 128:256]).astype(BF)
            return dq_low + both[0:128], dq_high + both[128:256]

        dq_low, dq_high = lax.fori_loop(0, 8, step, (jnp.zeros((128, n), F32), start_high))
        dk_all[0, 64:128, :] = tail_k.astype(BF)
        dv_all[0, 64:128, :] = tail_v.astype(BF)
        target = slice(128 * index, 128 * index + 64 * kv_heads)
        for pieces, whole, outer_first in (
            ((dk0, dk1, dk2, dk3, dk4), dk_all, True),
            ((dv0, dv1, dv2, dv3, dv4), dv_all, False),
        ):
            for chunk in range(32):
                one, two, zed = chunk // 8, (chunk // 2) % 4, chunk % 2
                outer, inner = (one, two) if outer_first else (two, one)
                if outer < 3:
                    piece, spot = pieces[outer], 2 * inner + zed
                else:
                    piece, spot = pieces[3 + inner // 2], 2 * (inner % 2) + zed
                piece[spot, :, target] = whole[chunk, :, 0 : 64 * kv_heads]
        for start, part in ((0, dq_low), (64, dq_high)):
            here = slice(start, start + 64)
            part = unspread_heads(part.T, kv_heads) * 0.125
            dq_ref[here, columns] = rotate_slabs(part, cos_ref[here, :], sin_ref[here, :]).astype(BF)


def place_rows(out_ref, starts, blocks):
    own, core, one, two, core_one, core_two = blocks
    for place, block, first, count in (
        (0, own, 0, 240),
        (1, core, 0, 240),
        (2, one, 0, 128),
        (2, two, 128, 112),
        (3, core_one, 0, 128),
        (3, core_two, 128, 112),
    ):
        rows = pl.ds(pl.multiple_of(starts[place] + first, 16), count)
        out_ref[rows, :] = block[...]


def project_kernel(starts, x_ref, gain_ref, cos_ref, sin_ref, b0, b1, b2, b3, b4, b5,
                   w_ref, n_ref, nt_ref, q_ref, kv_ref):
    place_rows(w_ref, starts, (b0, b1, b2, b3, b4, b5))
    x = x_ref[...].astype(F32)
    normed, _ = norm_forward(x, gain_ref[0:1, :])
    low = normed.astype(BF)
    n_ref[...] = low
    nt_ref[...] = low.astype(F32).T.astype(BF)
    product = matrix_product(low, w_ref[...])
    turned = rotate_slabs(product[:, 0:1280], cos_ref[...], sin_ref[...])
    q_ref[:, 0:960] = turned[:, 0:960].astype(BF)
    q_ref[:, 960:1024] = jnp.zeros((128, 64), BF)
    kv_ref[:, 0:320] = turned[:, 960:1280].astype(BF)
    kv_ref[:, 320:640] = product[:, 1280:1600].astype(BF)


def middle_kernel(starts, att_ref, x_ref, gain_ref, b0, b1, b2, b3, b4, b5, w_ref, mid_ref, n_ref, at_ref):
    place_rows(w_ref, starts, (b0, b1, b2, b3, b4, b5))
    low = att_ref[:, 0:960]
    at_ref[...] = low.astype(F32).T.astype(BF)
    middle = x_ref[...].astype(F32) + matrix_product(low, w_ref[...])
    mid_ref[...] = middle
    n_ref[...] = norm_forward(middle, gain_ref[1:2, :])[0].astype(BF)


def feed_forward_kernel(n0, n1, n2, n3, c0, c1, c2, c3, wg_ref, wu_ref, wd_ref,
                        pack_ref, dn_near, dn_far, y_near, y_far):
    normed = jnp.concatenate([n0[...], n1[...], n2[...], n3[...]], axis=0)
    upstream = jnp.concatenate([c0[...], c1[...], c2[...], c3[...]], axis=0)
    gate = matrix_product(normed, wg_ref[...])
    up = matrix_product(normed, wu_ref[...])
    grad_hidden = nt(upstream, wd_ref[...])
    sigmoid = 1.0 / (1.0 + jnp.exp(-gate))
    silu = gate * sigmoid
    hidden = (silu * up).astype(BF)
    grad_up = (grad_hidden * silu).astype(BF)
    grad_gate = (grad_hidden * up * sigmoid * (1.0 + gate * (1.0 - sigmoid))).astype(BF)
    back = (nt(grad_gate, wg_ref[...]) + nt(grad_up, wu_ref[...])).astype(BF)
    dn_near[...] = back[0:256].reshape(2, 128, 960)
    dn_far[...] = back[256:512].reshape(2, 128, 960)
    result = matrix_product(hidden, wd_ref[...]).astype(BF)
    y_near[...] = result[0:256].reshape(2, 128, 960)
    y_far[...] = result[256:512].reshape(2, 128, 960)
    for start, left, right in ((0, normed, grad_gate), (64, normed, grad_up), (128, upstream, hidden)):
        pack_ref[0:15, start : start + 64, :] = tn(left, right).astype(BF).reshape(15, 64, 640)
    pack_ref[15] = jnp.zeros((192, 640), BF)


def branch_kernel(own_ref, core_ref, mid_ref, gain_ref, cot_ref, w_ref, grad_ref, low_ref, d_ref, gain_out):
    d_normed = own_ref[...].astype(F32) + core_ref[...].astype(F32)
    middle = mid_ref[...]
    gain = gain_ref[1:2, :]
    inverse = lax.rsqrt(jnp.mean(middle * middle, axis=-1, keepdims=True) + EPSILON)
    weighted = d_normed * gain
    through = inverse * weighted - middle * inverse**3 * jnp.mean(weighted * middle, axis=-1, keepdims=True)
    gain_out[...] = jnp.sum(d_normed * middle * inverse, axis=0, keepdims=True)
    grad = cot_ref[...].astype(F32) + through
    grad_ref[...] = grad
    low = grad.astype(BF)
    low_ref[...] = low
    d_ref[:, 0:960] = nt(low, w_ref[...]).astype(BF)
    d_ref[:, 960:1024] = jnp.zeros((128, 64), BF)


def pass_on_kernel(*refs):
    for pair in range(2):
        left, right, from_left, from_right = refs[4 * pair : 4 * pair + 4]
        send_right, send_left = refs[8 + 2 * pair : 10 + 2 * pair]
        for chunk in range(8):
            if chunk < 4:
                send_right[chunk] = (right[chunk].astype(F32) + from_left[chunk].astype(F32)).astype(BF)
                send_left[chunk] = left[chunk]
            else:
                send_right[chunk] = right[chunk]
                send_left[chunk] = (left[chunk].astype(F32) + from_right[chunk - 4].astype(F32)).astype(BF)


def far_sum_kernel(*refs):
    for pair in range(2):
        own, one, two = refs[3 * pair : 3 * pair + 3]
        outs = refs[6 + 4 * pair : 10 + 4 * pair]
        for chunk in range(8):
            total = own[chunk].astype(F32) + one[chunk].astype(F32) + two[chunk].astype(F32)
            outs[chunk // 2][chunk % 2] = total.astype(BF)


def near_sum_kernel(*refs):
    own_ref, send_ref = refs[8:]
    for pair in range(2):
        lanes = slice(320 * pair, 320 * pair + 320)
        total = refs[4 * pair][...].astype(F32)
        for part in refs[4 * pair + 1 : 4 * pair + 4]:
            total = total + part[...].astype(F32)
        own_ref[:, lanes] = total[0]
        send_ref[:, lanes] = total[1].astype(BF)


def join_kernel(own_ref, other_ref, cos_ref, sin_ref, out_ref):
    total = own_ref[...] + other_ref[...].astype(F32)
    keys = rotate_slabs(total[:, 0:384], cos_ref[...], sin_ref[...])
    out_ref[:, 0:320] = keys[:, 0:320].astype(BF)
    out_ref[:, 320:640] = total[:, 320:640].astype(BF)


def weight_kernel(columns, b0, b1, b2, b3, e0, e1, e2, e3, g0, g1, g2, g3, gains_ref, out_ref):
    branch = jnp.concatenate([b0[...], b1[...], b2[...], b3[...]], axis=0)
    query = jnp.concatenate([e0[...], e1[...], e2[...], e3[...]], axis=0)
    late = jnp.concatenate([g0[...], g1[...], g2[...], g3[...]], axis=0)
    out_ref[0:240, 0:960] = matrix_product(columns[1], branch).astype(BF)
    out_ref[0:240, 960:1920] = matrix_product(columns[0], query).astype(BF)
    out_ref[0:240, 1920:2560] = matrix_product(columns[0], late).astype(BF)
    out_ref[240:256, :] = jnp.zeros((16, 2560), BF)
    row = lax.broadcasted_iota(jnp.int32, (16, 512), 0)
    out_ref[240:256, 0:512] = jnp.where(row == 0, jnp.broadcast_to(gains_ref[0:1, :], (16, 512)), 0.0).astype(BF)


VMEM_SPEC = pl.BlockSpec(memory_space=pltpu.VMEM)
SMEM_SPEC = pl.BlockSpec(memory_space=pltpu.SMEM)


def limit(megabytes):
    return pltpu.CompilerParams(vmem_limit_bytes=megabytes * 1024 * 1024)


def kv_scratch(lanes):
    return [pltpu.VMEM((2048, lanes), BF) for _ in range(4)] + [pltpu.VMEM((2048, 256), BF) for _ in range(2)]


def cost(products):
    return pl.CostEstimate(
        flops=products * 2 * 128 * 4096 * 64, bytes_accessed=6_000_000, transcendentals=128 * 2048 * 6
    )


def attention_forward(flags, queries, keys, values):
    return pl.pallas_call(
        forward_kernel,
        out_shape=(
            jax.ShapeDtypeStruct((128, 1024), BF),
            jax.ShapeDtypeStruct((2, 960, 128), F32),
            jax.ShapeDtypeStruct((8, 1024), F32),
        ),
        in_specs=[SMEM_SPEC] + [VMEM_SPEC] * 11,
        out_specs=(VMEM_SPEC,) * 3,
        scratch_shapes=kv_scratch(384)
        + [pltpu.VMEM((2048, 384), F32) for _ in range(2)]
        + [pltpu.VMEM((2048, 384), BF) for _ in range(2)],
        compiler_params=limit(30),
        cost_estimate=cost(60),
        name="attention_forward",
    )(flags, queries, *keys, *values)


def attention_backward(flags, queries, gradient, wide, stats, tables, keys, values):
    pieces = [jax.ShapeDtypeStruct((count, 128, 320), BF) for count in (8, 8, 8, 4, 4)] * 2
    out = pl.pallas_call(
        backward_kernel,
        out_shape=tuple([jax.ShapeDtypeStruct((128, 1024), BF)] + pieces),
        in_specs=[SMEM_SPEC] + [VMEM_SPEC] * 16,
        out_specs=(VMEM_SPEC,) * 11,
        scratch_shapes=kv_scratch(128) + [pltpu.VMEM((32, 128, 128), BF) for _ in range(2)],
        compiler_params=limit(24),
        cost_estimate=cost(120),
        name="attention_backward",
    )(flags, queries, gradient, wide, stats, *tables, *keys, *values)
    return out[0], out[1:6], out[6:11]


def unpack_kernel(pack_ref, gate_ref, up_ref, down_ref, done_ref):
    def part(start):
        return pack_ref[0:15, start : start + 64, :].astype(F32).reshape(960, 640)

    gate_ref[...] = part(0)
    up_ref[...] = part(64)
    down_ref[...] = part(128).T
    done_ref[...] = jnp.zeros((8, 128), F32)


def call(kernel, name, outs, *operands, scalars=0, room=12):
    return pl.pallas_call(
        kernel,
        out_shape=tuple(jax.ShapeDtypeStruct(shape, dtype) for shape, dtype in outs),
        in_specs=[SMEM_SPEC] * scalars + [VMEM_SPEC] * (len(operands) - scalars),
        out_specs=(VMEM_SPEC,) * len(outs),
        compiler_params=limit(room),
        name=name,
    )(*operands)


def context_scatter(keys, values, tables, later):
    block = lambda count: ((count, 128, 320), BF)
    far = ring_far(keys, values, "x", "y")
    sends = call(
        pass_on_kernel, "pass_on", (block(8),) * 4,
        keys[1], keys[2], far[0], far[1], values[1], values[2], far[2], far[3],
    )
    first, later = together(sends[0], later)
    got = (shift(first, "x", 1), shift(sends[1], "x", -1), shift(sends[2], "y", 1), shift(sends[3], "y", -1))
    parts = call(far_sum_kernel, "far_sum", (block(2),) * 8, keys[0], got[0], got[1], values[0], got[2], got[3])
    near = near_scatter(parts[:4], "y") + near_scatter(parts[4:], "x")
    own, send = call(near_sum_kernel, "near_sum", (((128, 640), F32), ((128, 640), BF)), *near)
    return call(join_kernel, "join", (((128, 640), BF),), own, shift(send, "zh", 1), *tables)[0], later


def weight_gradients(columns, branch, query, late, gains):
    return pl.pallas_call(
        weight_kernel,
        out_shape=jax.ShapeDtypeStruct((256, 2560), BF),
        in_specs=[VMEM_SPEC] * 14,
        out_specs=VMEM_SPEC,
        compiler_params=limit(16),
        name="weight_gradients",
    )(columns, *branch, *query, *late, gains)


def body(
    tokens, block_pairs, w_query, key_weight, value_weight, w_out, gain_attn, gain_mlp, w_gate, w_up, w_down, cotangent
):
    rows, width = tokens.shape[1:]
    kv_width = KEY_VALUE_HEADS * HEAD_SIZE
    x_here, y_here, z_here = lax.axis_index("x"), lax.axis_index("y"), lax.axis_index("zh")
    place = 2 * lax.axis_index("zl") + lax.axis_index("co")
    context = z_here * 16 + x_here * 4 + y_here

    in_blocks = weight_blocks(jnp.concatenate([w_query, key_weight, value_weight], axis=1))
    gains = lax.all_gather(jnp.stack([gain_attn, gain_mlp])[None], FS, axis=0, tiled=True)
    gains = jnp.swapaxes(gains, 0, 1).reshape(2, width).astype(F32)
    starts = jnp.stack([place, place ^ 1, place ^ 2, place ^ 3]).astype(jnp.int32) * (width // 4)

    order = [
        ((z_here + z) % 2) * 16 + ((x_here + x + 4) % 4) * 4 + (y_here + y + 4) % 4
        for x in RING
        for y in RING
        for z in (0, 1)
    ]
    pairs = block_pairs[0][jnp.stack(order)]
    flags = jnp.where(jnp.arange(32) == 0, 1, (pairs < pairs[0]).astype(jnp.int32))
    offsets = jnp.arange(rows // 2, dtype=jnp.int32)
    query_places = jnp.concatenate(
        [pairs[0] * (rows // 2) + offsets, (63 - pairs[0]) * (rows // 2) + offsets]
    )
    frequency = 10000.0 ** (-jnp.arange(HEAD_SIZE // 2, dtype=F32) / (HEAD_SIZE // 2))
    angles = query_places.astype(F32)[:, None] * frequency[None, :]
    cosine, sine = jnp.cos(angles), jnp.sin(angles)
    cosine = jnp.concatenate([cosine] * 4, axis=1)
    sine = jnp.concatenate([-sine, sine] * 2, axis=1)
    tables = (cosine, -sine)

    weights_in, normed_low, normed_turned, flat_queries, kv = call(
        project_kernel,
        "project",
        (((width, 1600), BF), ((rows, width), BF), ((width, rows), BF), ((rows, 1024), BF), ((rows, 640), BF)),
        starts, tokens[0], gains, cosine, sine, *in_blocks, scalars=1, room=16,
    )
    all_keys, all_values = context_gather(kv)
    late_out, late_cotangent, own_keys = together(w_out, cotangent[0], all_keys[0])
    all_keys = (own_keys, *all_keys[1:])
    out_blocks = weight_blocks(late_out)
    upstream_blocks = pair_blocks(late_cotangent)
    attended_low, attended_wide, stats = attention_forward(flags, flat_queries, all_keys, all_values)
    out_w, middle, normed_two, attended_turned = call(
        middle_kernel,
        "middle",
        (((width, width), BF), ((rows, width), F32), ((rows, width), BF), ((width, rows), BF)),
        starts, attended_low, tokens[0], gains, *out_blocks, scalars=1,
    )
    half = ((2, rows, width), BF)
    pack, dn_near, dn_far, y_near, y_far = call(
        feed_forward_kernel,
        "feed_forward",
        (((16, 192, w_gate.shape[1]), BF), half, half, half, half),
        *pair_blocks(normed_two), *upstream_blocks, w_gate, w_up, w_down, room=26,
    )
    near = add_low(dn_near, shift(dn_far, "zl", 1))
    grad_middle, grad_branch, attended_gradient, grad_gain_two = call(
        branch_kernel,
        "branch",
        (((rows, width), F32), ((rows, width), BF), ((rows, 1024), BF), ((1, width), F32)),
        near[0], shift(near[1], "co", 1), middle, gains, cotangent[0], out_w,
    )

    back = (flat_queries, attended_gradient, attended_wide, stats, tables, all_keys, all_values)
    quarter = width // 4
    pack_slots = lax.all_to_all(pack, ("x", "y"), 0, 0, tiled=True)
    columns = jnp.stack(
        [normed_turned.reshape(4, quarter, rows), attended_turned.reshape(4, quarter, rows)], axis=1
    )
    columns = column_exchange(columns, place)
    all_branch = pair_blocks(grad_branch)
    grad_query_pre, key_parts, value_parts = attention_backward(flags, *back)
    grad_kv, pack_slots = context_scatter(key_parts, value_parts, tables, pack_slots)
    pack_slot = jnp.sum(pack_slots.astype(F32), axis=0).astype(BF)
    pack_slot = add_low(pack_slot, shift(pack_slot, "zh", 1))
    pack_all = lax.all_gather(pack_slot[None], ("x", "y"), axis=0, tiled=True)
    grad_query_pre = grad_query_pre[:, :width]
    late = pair_blocks(grad_kv)
    y_near, y_far, grad_kv = together(y_near, y_far, grad_kv)
    near = add_low(y_near, shift(y_far, "zl", 1))
    mlp_term = near[0].astype(F32) + shift(near[1], "co", 1).astype(F32)
    result = (middle + mlp_term).astype(BF)[None]
    all_query = pair_blocks(grad_query_pre)
    grad_normed_one = right_inner(jnp.concatenate([grad_query_pre, grad_kv], axis=1), weights_in)
    inputs = tokens[0].astype(F32)
    inverse_one = norm_forward(inputs, gains[0])[1]
    through_one, grad_gain_one = norm_backward(inputs, inverse_one, gains[0], grad_normed_one)
    input_grad = (grad_middle + through_one)[None]

    grad_gains = jnp.stack([grad_gain_one, grad_gain_two[0]]).reshape(2, 4, 1, quarter)
    gain_parts = [
        lax.dynamic_index_in_dim(grad_gains, place ^ mask, axis=1, keepdims=False) for mask in range(4)
    ]
    near_gains = jnp.stack(gain_parts[:2]) + shift(jnp.stack(gain_parts[2:]), "zl", 1)
    gains_row = (near_gains[0] + shift(near_gains[1], "co", 1)).reshape(1, 2 * quarter)
    last = weight_gradients(columns, all_branch, all_query, late, jnp.pad(gains_row, ((0, 0), (0, 512 - 2 * quarter))))
    out = slot_sum(last.reshape(16, 16, -1), ("x", "y")).astype(BF)
    out = add_low(out, shift(out, "zh", 1))
    hidden = w_gate.shape[1]
    gate_sum, up_sum, down_sum, done = call(
        unpack_kernel,
        "unpack",
        (((width, hidden), F32), ((width, hidden), F32), ((hidden, width), F32), ((8, 128), F32)),
        pack_all, room=24,
    )
    out = (out.astype(F32) + done[0, 0]).astype(BF)
    sum_last = slot_gather(out, ("x", "y")).reshape(256, -1)

    return (
        result,
        input_grad,
        sum_last[:quarter, width : 2 * width].astype(F32),
        sum_last[:quarter, 2 * width : 2 * width + kv_width].astype(F32),
        sum_last[:quarter, 2 * width + kv_width :].astype(F32),
        sum_last[:quarter, :width].astype(F32),
        sum_last[quarter, :quarter].astype(F32),
        sum_last[quarter, quarter : 2 * quarter].astype(F32),
        gate_sum,
        up_sum,
        down_sum,
    )


def solution(mesh):
    split = Mesh(mesh.devices.reshape(2, 4, 4, 2, 2), ("zh", "x", "y", "zl", "co"))
    ctx = ("zh", "x", "y")
    in_specs = (
        P(FS, ctx, None),
        P(FS, None),
        P(FS, None),
        P(FS, None),
        P(FS, None),
        P(FS, None),
        P(FS),
        P(FS),
        P(None, FS),
        P(None, FS),
        P(FS, None),
        P(FS, ctx, None),
    )
    out_specs = (
        P(FS, ctx, None),
        P(FS, ctx, None),
        P(FS, None),
        P(FS, None),
        P(FS, None),
        P(FS, None),
        P(FS),
        P(FS),
        P(None, FS),
        P(None, FS),
        P(FS, None),
    )
    return jax.shard_map(body, mesh=split, in_specs=in_specs, out_specs=out_specs, check_vma=False)
```

```python
import functools

import jax
import jax.numpy as jnp
from jax import lax
from jax.experimental import pallas as pl
from jax.experimental.pallas import tpu as pltpu
from jax.sharding import Mesh, PartitionSpec as P

QUERY_HEADS = 15
KEY_VALUE_HEADS = 5
HEAD_SIZE = 64
EPSILON = 1e-05
BF = jnp.bfloat16
F32 = jnp.float32
FS = ("zl", "co")
RING = (0, -1, 1, 2)


def matrix_product(left, right):
    return jnp.dot(left, right, preferred_element_type=F32)


def left_inner(left, right):
    return lax.dot_general(left, right, (((0,), (0,)), ((), ())), preferred_element_type=F32)


def right_inner(left, right):
    return lax.dot_general(left, right, (((1,), (1,)), ((), ())), preferred_element_type=F32)


def shift(value, axis, step):
    count = lax.axis_size(axis)
    return lax.ppermute(value, axis, [(i, (i + step) % count) for i in range(count)])


def add_low(*parts):
    total = parts[0].astype(F32)
    for part in parts[1:]:
        total = total + part.astype(F32)
    return total.astype(BF)


def together(*values):
    return lax.optimization_barrier(values)


def ring_pick(value, axis):
    here = lax.axis_index(axis)
    return [
        lax.dynamic_index_in_dim(value, lax.rem(here + off + 4, 4), axis=0, keepdims=False) for off in RING
    ]


def ring_place(blocks, axis):
    here = lax.axis_index(axis)
    out = jnp.stack(blocks)
    for block, off in zip(blocks, RING):
        out = lax.dynamic_update_slice_in_dim(out, block[None], lax.rem(here + off + 4, 4), axis=0)
    return out


def near_gather(value, axis):
    return [value, shift(value, axis, 1), shift(value, axis, -1), shift(value, axis, 2)]


def near_scatter(blocks, axis):
    return [blocks[0], shift(blocks[1], axis, -1), shift(blocks[2], axis, 1), shift(blocks[3], axis, 2)]


def two_ring_gather(one, two, axis_one, axis_two):
    left_one, right_one, left_two, right_two = (
        shift(one, axis_one, 1), shift(one, axis_one, -1), shift(two, axis_two, 1), shift(two, axis_two, -1)
    )
    half = one.shape[0] // 2
    far = (
        shift(left_one[:half], axis_one, 1),
        shift(right_one[half:], axis_one, -1),
        shift(left_two[:half], axis_two, 1),
        shift(right_two[half:], axis_two, -1),
    )
    return (one, left_one, right_one, far[0], far[1]), (two, left_two, right_two, far[2], far[3])


def ring_far(one, two, axis_one, axis_two):
    return (
        shift(one[3], axis_one, 1), shift(one[4], axis_one, -1), shift(two[3], axis_two, 1), shift(two[4], axis_two, -1)
    )


def pair_gather(value):
    both = jnp.concatenate([value[None], shift(value, "zl", 1)[None]], axis=0)
    other = shift(both, "co", 1)
    return jnp.stack([both[0], other[0], both[1], other[1]])


def pair_blocks(value):
    far = shift(value, "zl", 1)
    return value, shift(value, "co", 1), far, shift(far, "co", 1)


def near_blocks(value):
    return tuple(lax.ppermute(value, FS, [(i, i ^ mask) for i in range(4)]) if mask else value for mask in range(4))


def pair_scatter(value):
    near = add_low(value[:2], shift(value[2:].astype(BF), "zl", 1))
    return near[0].astype(F32) + shift(near[1], "co", 1).astype(F32)


def weight_blocks(value):
    cut = 128
    zed = ("zh", "zl")
    one = shift(value[:cut], zed, 1)
    two = shift(value[cut:], zed, -1)
    return value, shift(value, "co", 1), one, two, shift(one, "co", 1), shift(two, "co", 1)


def context_gather(both):
    other = shift(both, "zh", 1)
    keys = jnp.concatenate(near_gather(jnp.stack([both[0], other[0]]), "y"))
    values = jnp.concatenate(near_gather(jnp.stack([both[1], other[1]]), "x"))
    return two_ring_gather(keys, values, "x", "y")


def slot_sum(value, axes):
    parts = lax.all_to_all(value, axes, 0, 0, tiled=True)
    return jnp.sum(parts.astype(F32), axis=0)


def slot_gather(value, axes):
    count = lax.axis_size(axes)
    return lax.all_to_all(jnp.broadcast_to(value[None], (count,) + value.shape), axes, 0, 0, tiled=True)


def column_exchange(value, place):
    parts = []
    for mask in range(4):
        part = lax.dynamic_index_in_dim(value, place ^ mask, axis=0, keepdims=False)
        parts.append(lax.ppermute(part, FS, [(i, i ^ mask) for i in range(4)]) if mask else part)
    return parts


def apply_rotation(values, cosine_table, sinusoid_table):
    half = values.shape[-1] // 2
    leading, trailing = values[..., :half], values[..., half:]
    return jnp.concatenate(
        [
            leading * cosine_table - trailing * sinusoid_table,
            trailing * cosine_table + leading * sinusoid_table,
        ],
        axis=-1,
    )


def norm_forward(values, gain_vector):
    inverse = lax.rsqrt(jnp.mean(values * values, axis=-1, keepdims=True) + EPSILON)
    return (values * inverse * gain_vector, inverse)


def norm_backward(values, inverse, gain_vector, gradient):
    weighted = gradient * gain_vector
    through = inverse * weighted - values * inverse**3 * jnp.mean(
        weighted * values, axis=-1, keepdims=True
    )
    return (through, jnp.sum(gradient * values * inverse, axis=0))


HEAD_GROUPS = ((0, 2), (1, 2), (2, 1))
NEGATIVE = -1e30


def nt(left, right):
    return lax.dot_general(left, right, (((1,), (1,)), ((), ())), preferred_element_type=F32)


def tn(left, right):
    return lax.dot_general(left, right, (((0,), (0,)), ((), ())), preferred_element_type=F32)


def swap_halves(slab):
    return jnp.concatenate([slab[:, 64:], slab[:, :64]], axis=1)


def spread_heads(rows, kv_heads):
    lane = lax.broadcasted_iota(jnp.int32, (64, 128), 1)
    blocks = []
    for kv in range(kv_heads):
        for group in range(3):
            head = 3 * kv + group
            slab = rows[:, 128 * (head // 2) : 128 * (head // 2) + 128]
            if head % 2 != kv:
                slab = swap_halves(slab)
            blocks.append(jnp.where((lane < 64) == (kv == 0), slab, 0.0))
    return jnp.concatenate(blocks, axis=0)


def unspread_heads(blocks, kv_heads):
    lane = lax.broadcasted_iota(jnp.int32, (64, 128), 1)
    count = 3 * kv_heads
    slabs = []
    for slab in range((count + 1) // 2):
        halves = []
        for side in range(2):
            head = 2 * slab + side
            if head >= count:
                halves.append(jnp.zeros((64, 128), F32))
                continue
            block = blocks[64 * head : 64 * head + 64]
            halves.append(block if head // 3 == side else swap_halves(block))
        slabs.append(jnp.where(lane < 64, halves[0], halves[1]))
    return jnp.concatenate(slabs, axis=1)


def causal_mask(columns):
    key = lax.broadcasted_iota(jnp.int32, (64, columns), 0)
    query = lax.rem(lax.broadcasted_iota(jnp.int32, (64, columns), 1), 64)
    return key <= query


def fill_chunks(pieces, low, high, outer_first, index, width):
    if width % 128:
        zeros = jnp.zeros((2048, 64), BF)
        low[:, width : width + 64] = zeros
        high[:, width : width + 64] = zeros
    start = 256 * index
    for chunk in range(32):
        one, two, zed = chunk // 8, (chunk // 2) % 4, chunk % 2
        outer, inner = (one, two) if outer_first else (two, one)
        if outer < 3:
            block = pieces[outer].at[2 * inner + zed]
        else:
            block = pieces[3 + inner // 2].at[2 * (inner % 2) + zed]
        low[64 * chunk : 64 * chunk + 64, 0:width] = block[:, start : start + width]
        high[64 * chunk : 64 * chunk + 64, 0:width] = block[:, start + width : start + 2 * width]


def blocks_beside(value):
    low, high = value[0:64], value[64:128]
    return jnp.concatenate(
        [low[:, 0:128], high[:, 0:128], low[:, 128:256], high[:, 128:256], low[:, 256:320], high[:, 256:320]], axis=1
    )


def blocks_apart(value):
    low = jnp.concatenate([value[:, 0:128], value[:, 256:384], value[:, 512:640]], axis=1)
    high = jnp.concatenate([value[:, 128:256], value[:, 384:512], swap_halves(value[:, 512:640])], axis=1)
    return jnp.concatenate([low, high], axis=0)


def mix_chunks(flags, low, high, mixed, lanes):
    def step(chunk, carry):
        rows = pl.ds(pl.multiple_of(chunk * 64, 64), 64)
        chosen = flags[chunk] > 0
        mixed[rows, 0:128] = jnp.where(chosen, low[rows, lanes], jnp.zeros((64, 128), BF))
        mixed[rows, 128:256] = jnp.where(chosen, jnp.zeros((64, 128), BF), high[rows, lanes])
        return carry

    lax.fori_loop(0, 32, step, 0)


def fold_rows(value, op):
    parts = value.reshape(value.shape[0] // 8, 8, value.shape[1])
    return op(parts, axis=0)


def forward_kernel(flags, q_ref, k0, k1, k2, k3, k4, v0, v1, v2, v3, v4, att_ref, wide_ref, stat_ref,
                   k_low, k_high, v_low, v_high, k_mix, v_mix, s_one, s_two, p_one, p_two):
    stat_ref[...] = jnp.zeros(stat_ref.shape, F32)
    lanes = slice(0, 128)
    for index, kv_heads in HEAD_GROUPS:
        fill_chunks((k0, k1, k2, k3, k4), k_low, k_high, True, index, 64 * kv_heads)
        fill_chunks((v0, v1, v2, v3, v4), v_low, v_high, False, index, 64 * kv_heads)
        n = 192 * kv_heads
        wide = 128 * ((3 * kv_heads + 1) // 2)
        columns = slice(384 * index, 384 * index + wide)
        q_all = q_ref[:, columns].astype(F32) * 0.125
        q_low = spread_heads(q_all[0:64], kv_heads).astype(BF)
        q_high = spread_heads(q_all[64:128], kv_heads).astype(BF)
        q_both = jnp.concatenate([q_low, q_high], axis=1)
        mix_chunks(flags, k_low, k_high, k_mix, lanes)
        mix_chunks(flags, v_low, v_high, v_mix, lanes)
        allowed = causal_mask(n)
        tail = jnp.where(allowed, nt(k_high[0:64, lanes], q_high), NEGATIVE)
        floor = jnp.full((8, n), NEGATIVE, F32)

        def scores(block, carry):
            max_low, max_high = carry
            rows = pl.ds(pl.multiple_of(block * 256, 256), 256)
            one = nt(k_low[rows, lanes], q_high)
            s_one[rows, 0:n] = one
            max_high = jnp.maximum(max_high, fold_rows(one, jnp.max))
            two = nt(k_mix[rows, :], q_both)
            first = jnp.where(jnp.logical_or(allowed, block > 0), two[0:64], NEGATIVE)
            two = jnp.concatenate([first, two[64:]], axis=0)
            s_two[rows, 0:n] = two
            for part in range(4):
                top = fold_rows(two[64 * part : 64 * part + 64], jnp.max)
                chosen = flags[block * 4 + part] > 0
                max_low = jnp.maximum(max_low, jnp.where(chosen, top, NEGATIVE))
                max_high = jnp.maximum(max_high, jnp.where(chosen, NEGATIVE, top))
            return max_low, max_high

        max_low, max_high = lax.fori_loop(0, 8, scores, (floor, fold_rows(tail, jnp.max)))
        max_low = jnp.max(max_low, axis=0, keepdims=True)
        max_high = jnp.max(max_high, axis=0, keepdims=True)
        tail = jnp.exp(tail - max_high)

        def weights(block, carry):
            sum_low, sum_high = carry
            rows = pl.ds(pl.multiple_of(block * 256, 256), 256)
            one = jnp.exp(s_one[rows, 0:n] - max_high)
            p_one[rows, 0:n] = one.astype(BF)
            sum_high = sum_high + fold_rows(one, jnp.sum)
            for part in range(4):
                chosen = flags[block * 4 + part] > 0
                small = pl.ds(pl.multiple_of(block * 256 + 64 * part, 64), 64)
                two = jnp.exp(s_two[small, 0:n] - jnp.where(chosen, max_low, max_high))
                p_two[small, 0:n] = two.astype(BF)
                total = fold_rows(two, jnp.sum)
                sum_low = sum_low + jnp.where(chosen, total, 0.0)
                sum_high = sum_high + jnp.where(chosen, 0.0, total)
            return sum_low, sum_high

        sum_low, sum_high = lax.fori_loop(
            0, 8, weights, (jnp.zeros((8, n), F32), fold_rows(tail, jnp.sum))
        )
        sum_low = jnp.sum(sum_low, axis=0, keepdims=True)
        sum_high = jnp.sum(sum_high, axis=0, keepdims=True)
        out_two = tn(v_mix[...], p_two[:, 0:n])
        out_high = tn(v_low[:, lanes], p_one[:, 0:n]) + out_two[128:256]
        out_high = (out_high + tn(v_high[0:64, lanes], tail.astype(BF))) / sum_high
        out_low = out_two[0:128] / sum_low
        out_low, out_high = out_low.T, out_high.T
        span = slice(384 * index, 384 * index + n)
        wide_ref[0, span, :] = out_low
        wide_ref[1, span, :] = out_high
        att_ref[0:64, columns] = unspread_heads(out_low, kv_heads).astype(BF)
        att_ref[64:128, columns] = unspread_heads(out_high, kv_heads).astype(BF)
        stat_ref[0:1, span] = max_low + jnp.log(sum_low)
        stat_ref[1:2, span] = max_high + jnp.log(sum_high)


def rotate_slabs(value, cosine, sine):
    lane = lax.broadcasted_iota(jnp.int32, (value.shape[0], 128), 1)
    slabs = []
    for start in range(0, value.shape[1], 128):
        slab = value[:, start : start + 128]
        other = jnp.where(lane % 64 < 32, pltpu.roll(slab, 96, 1), pltpu.roll(slab, 32, 1))
        slabs.append(slab * cosine + other * sine)
    return jnp.concatenate(slabs, axis=1)


def backward_kernel(flags, q_ref, d_ref, wide_ref, stat_ref, cos_ref, sin_ref,
                    k0, k1, k2, k3, k4, v0, v1, v2, v3, v4,
                    dq_ref, dk0, dk1, dk2, dk3, dk4, dv0, dv1, dv2, dv3, dv4,
                    k_low, k_high, v_low, v_high, k_mix, v_mix, dk_all, dv_all):
    for index, kv_heads in HEAD_GROUPS:
        fill_chunks((k0, k1, k2, k3, k4), k_low, k_high, True, index, 64 * kv_heads)
        fill_chunks((v0, v1, v2, v3, v4), v_low, v_high, False, index, 64 * kv_heads)
        lanes = slice(0, 128)
        n = 192 * kv_heads
        wide = 128 * ((3 * kv_heads + 1) // 2)
        columns = slice(384 * index, 384 * index + wide)
        span = slice(384 * index, 384 * index + n)
        q_all = q_ref[:, columns].astype(F32) * 0.125
        d_all = d_ref[:, columns].astype(F32)
        q_low = spread_heads(q_all[0:64], kv_heads).astype(BF)
        q_high = spread_heads(q_all[64:128], kv_heads).astype(BF)
        q_both = jnp.concatenate([q_low, q_high], axis=1)
        d_low = spread_heads(d_all[0:64], kv_heads)
        d_high = spread_heads(d_all[64:128], kv_heads)
        ones = jnp.ones((8, 128), F32)

        def row_sums(value):
            return lax.dot_general(
                ones, value, (((1,), (1,)), ((), ())),
                precision=lax.Precision.HIGHEST, preferred_element_type=F32,
            )[0:1]

        delta_low = row_sums(d_low * wide_ref[0, span, :])
        delta_high = row_sums(d_high * wide_ref[1, span, :])
        d_low, d_high = d_low.astype(BF), d_high.astype(BF)
        d_both = jnp.concatenate([d_low, d_high], axis=1)
        log_low, log_high = stat_ref[0:1, span], stat_ref[1:2, span]
        mix_chunks(flags, k_low, k_high, k_mix, lanes)
        mix_chunks(flags, v_low, v_high, v_mix, lanes)
        allowed = causal_mask(n)

        own_k, own_v = k_high[0:64, lanes], v_high[0:64, lanes]
        soft = jnp.where(allowed, jnp.exp(nt(own_k, q_high) - log_high), 0.0)
        grad = (soft * (nt(own_v, d_high) - delta_high)).astype(BF)
        tail_k = matrix_product(grad, q_high)
        tail_v = matrix_product(soft.astype(BF), d_high)
        start_high = tn(own_k, grad)

        def step(block, carry):
            dq_low, dq_high = carry
            rows = pl.ds(pl.multiple_of(block * 256, 256), 256)
            k_one, v_one = k_low[rows, lanes], v_low[rows, lanes]
            soft = jnp.exp(nt(k_one, q_high) - log_high)
            grad = (soft * (nt(v_one, d_high) - delta_high)).astype(BF)
            dk_one = matrix_product(grad, q_high)
            dv_one = matrix_product(soft.astype(BF), d_high)
            dq_high = dq_high + tn(k_one, grad)
            k_two, v_two = k_mix[rows, :], v_mix[rows, :]
            two = nt(k_two, q_both)
            two_grad = nt(v_two, d_both)
            softs, grads = [], []
            for part in range(4):
                chosen = flags[block * 4 + part] > 0
                inner = slice(64 * part, 64 * part + 64)
                soft = jnp.exp(two[inner] - jnp.where(chosen, log_low, log_high))
                if part == 0:
                    soft = jnp.where(jnp.logical_or(allowed, block > 0), soft, 0.0)
                softs.append(soft.astype(BF))
                grads.append(
                    (soft * (two_grad[inner] - jnp.where(chosen, delta_low, delta_high))).astype(BF)
                )
            soft = jnp.concatenate(softs, axis=0)
            grad = jnp.concatenate(grads, axis=0)
            dk_two = matrix_product(grad, q_both)
            dv_two = matrix_product(soft, d_both)
            both = tn(k_two, grad)
            for part in range(4):
                chosen = flags[block * 4 + part] > 0
                inner = slice(64 * part, 64 * part + 64)
                chunk = block * 4 + part
                for one, other, out in ((dk_one, dk_two, dk_all), (dv_one, dv_two, dv_all)):
                    out[chunk, 0:64, :] = (one[inner] + jnp.where(chosen, other[inner, 0:128], 0.0)).astype(BF)
                    out[chunk, 64:128, :] = jnp.where(chosen, 0.0, other[inner, 128:256]).astype(BF)
            return dq_low + both[0:128], dq_high + both[128:256]

        dq_low, dq_high = lax.fori_loop(0, 8, step, (jnp.zeros((128, n), F32), start_high))
        dk_all[0, 64:128, :] = tail_k.astype(BF)
        dv_all[0, 64:128, :] = tail_v.astype(BF)
        width, start = 64 * kv_heads, 256 * index
        for pieces, whole, outer_first in (
            ((dk0, dk1, dk2, dk3, dk4), dk_all, True),
            ((dv0, dv1, dv2, dv3, dv4), dv_all, False),
        ):
            for chunk in range(32):
                one, two, zed = chunk // 8, (chunk // 2) % 4, chunk % 2
                outer, inner = (one, two) if outer_first else (two, one)
                if outer < 3:
                    piece, spot = pieces[outer], 2 * inner + zed
                else:
                    piece, spot = pieces[3 + inner // 2], 2 * (inner % 2) + zed
                piece[spot, :, start : start + width] = whole[chunk, 0:64, 0:width]
                piece[spot, :, start + width : start + 2 * width] = whole[chunk, 64:128, 0:width]
        for start, part in ((0, dq_low), (64, dq_high)):
            here = slice(start, start + 64)
            part = unspread_heads(part.T, kv_heads) * 0.125
            dq_ref[here, columns] = rotate_slabs(part, cos_ref[here, :], sin_ref[here, :]).astype(BF)


def place_rows(out_ref, starts, blocks):
    own, core, one, two, core_one, core_two = blocks
    for place, block, first, count in (
        (0, own, 0, 240),
        (1, core, 0, 240),
        (2, one, 0, 128),
        (2, two, 128, 112),
        (3, core_one, 0, 128),
        (3, core_two, 128, 112),
    ):
        rows = pl.ds(pl.multiple_of(starts[place] + first, 16), count)
        out_ref[rows, :] = block[...]


def project_kernel(starts, x_ref, gain_ref, cos_ref, sin_ref, b0, b1, b2, b3, b4, b5,
                   w_ref, n_ref, nt_ref, q_ref, kv_ref):
    place_rows(w_ref, starts, (b0, b1, b2, b3, b4, b5))
    x = x_ref[...].astype(F32)
    normed, _ = norm_forward(x, gain_ref[0:1, :])
    low = normed.astype(BF)
    n_ref[...] = low
    nt_ref[...] = low.astype(F32).T.astype(BF)
    product = matrix_product(low, w_ref[...])
    turned = rotate_slabs(product[:, 0:1280], cos_ref[...], sin_ref[...])
    q_ref[:, 0:960] = turned[:, 0:960].astype(BF)
    q_ref[:, 960:1024] = jnp.zeros((128, 64), BF)
    kv_ref[0] = blocks_beside(turned[:, 960:1280]).astype(BF)
    kv_ref[1] = blocks_beside(product[:, 1280:1600]).astype(BF)


def middle_kernel(starts, att_ref, x_ref, gain_ref, b0, b1, b2, b3, b4, b5, w_ref, mid_ref, n_ref, at_ref):
    place_rows(w_ref, starts, (b0, b1, b2, b3, b4, b5))
    low = att_ref[:, 0:960]
    at_ref[...] = low.astype(F32).T.astype(BF)
    middle = x_ref[...].astype(F32) + matrix_product(low, w_ref[...])
    mid_ref[...] = middle
    n_ref[...] = norm_forward(middle, gain_ref[1:2, :])[0].astype(BF)


def feed_forward_kernel(n0, n1, n2, n3, c0, c1, c2, c3, wg_ref, wu_ref, wd_ref,
                        pack_ref, dn_near, dn_far, y_near, y_far):
    normed = jnp.concatenate([n0[...], n1[...], n2[...], n3[...]], axis=0)
    upstream = jnp.concatenate([c0[...], c1[...], c2[...], c3[...]], axis=0)
    gate = matrix_product(normed, wg_ref[...])
    up = matrix_product(normed, wu_ref[...])
    grad_hidden = matrix_product(upstream, wd_ref[...])
    sigmoid = 1.0 / (1.0 + jnp.exp(-gate))
    silu = gate * sigmoid
    hidden = (silu * up).astype(BF)
    grad_up = (grad_hidden * silu).astype(BF)
    grad_gate = (grad_hidden * up * sigmoid * (1.0 + gate * (1.0 - sigmoid))).astype(BF)
    back = (nt(grad_gate, wg_ref[...]) + nt(grad_up, wu_ref[...])).astype(BF)
    dn_near[...] = back[0:256].reshape(2, 128, 960)
    dn_far[...] = back[256:512].reshape(2, 128, 960)
    result = nt(hidden, wd_ref[...]).astype(BF)
    y_near[...] = result[0:256].reshape(2, 128, 960)
    y_far[...] = result[256:512].reshape(2, 128, 960)
    for start, left, right in ((0, normed, grad_gate), (64, normed, grad_up), (128, upstream, hidden)):
        pack_ref[0:15, start : start + 64, :] = tn(left, right).astype(BF).reshape(15, 64, 640)
    pack_ref[15] = jnp.zeros((192, 640), BF)


def branch_kernel(own_ref, core_ref, mid_ref, gain_ref, cot_ref, w_ref, grad_ref, low_ref, d_ref, gain_out):
    d_normed = own_ref[...].astype(F32) + core_ref[...].astype(F32)
    middle = mid_ref[...]
    gain = gain_ref[1:2, :]
    inverse = lax.rsqrt(jnp.mean(middle * middle, axis=-1, keepdims=True) + EPSILON)
    weighted = d_normed * gain
    through = inverse * weighted - middle * inverse**3 * jnp.mean(weighted * middle, axis=-1, keepdims=True)
    gain_out[...] = jnp.sum(d_normed * middle * inverse, axis=0, keepdims=True)
    grad = cot_ref[...].astype(F32) + through
    grad_ref[...] = grad
    low = grad.astype(BF)
    low_ref[...] = low
    d_ref[:, 0:960] = nt(low, w_ref[...]).astype(BF)
    d_ref[:, 960:1024] = jnp.zeros((128, 64), BF)


def pass_on_kernel(*refs):
    for pair in range(2):
        left, right, from_left, from_right = refs[4 * pair : 4 * pair + 4]
        send_right, send_left = refs[8 + 2 * pair : 10 + 2 * pair]
        for chunk in range(8):
            if chunk < 4:
                send_right[chunk] = (right[chunk].astype(F32) + from_left[chunk].astype(F32)).astype(BF)
                send_left[chunk] = left[chunk]
            else:
                send_right[chunk] = right[chunk]
                send_left[chunk] = (left[chunk].astype(F32) + from_right[chunk - 4].astype(F32)).astype(BF)


def far_sum_kernel(*refs):
    for pair in range(2):
        own, one, two = refs[3 * pair : 3 * pair + 3]
        outs = refs[6 + 4 * pair : 10 + 4 * pair]
        for chunk in range(8):
            total = own[chunk].astype(F32) + one[chunk].astype(F32) + two[chunk].astype(F32)
            outs[chunk // 2][chunk % 2] = total.astype(BF)


def near_sum_kernel(*refs):
    own_ref, send_ref = refs[8:]
    for pair in range(2):
        total = refs[4 * pair][...].astype(F32)
        for part in refs[4 * pair + 1 : 4 * pair + 4]:
            total = total + part[...].astype(F32)
        own_ref[pair] = total[0]
        send_ref[pair] = total[1].astype(BF)


def join_kernel(own_ref, other_ref, cos_ref, sin_ref, out_ref):
    total = own_ref[...] + other_ref[...].astype(F32)
    keys = rotate_slabs(blocks_apart(total[0]), cos_ref[...], sin_ref[...])
    out_ref[:, 0:320] = keys[:, 0:320].astype(BF)
    out_ref[:, 320:640] = blocks_apart(total[1])[:, 0:320].astype(BF)


def weight_kernel(c0, c1, c2, c3, b0, b1, b2, b3, e0, e1, e2, e3, g0, g1, g2, g3, gains_ref, out_ref):
    columns = [jnp.concatenate([c[place] for c in (c0, c1, c2, c3)], axis=1) for place in range(2)]
    branch = jnp.concatenate([b0[...], b1[...], b2[...], b3[...]], axis=0)
    query = jnp.concatenate([e0[...], e1[...], e2[...], e3[...]], axis=0)
    late = jnp.concatenate([g0[...], g1[...], g2[...], g3[...]], axis=0)
    out_ref[0:240, 0:960] = matrix_product(columns[1], branch).astype(BF)
    out_ref[0:240, 960:1920] = matrix_product(columns[0], query).astype(BF)
    out_ref[0:240, 1920:2560] = matrix_product(columns[0], late).astype(BF)
    out_ref[240:256, :] = jnp.zeros((16, 2560), BF)
    row = lax.broadcasted_iota(jnp.int32, (16, 512), 0)
    out_ref[240:256, 0:512] = jnp.where(row == 0, jnp.broadcast_to(gains_ref[0:1, :], (16, 512)), 0.0).astype(BF)


VMEM_SPEC = pl.BlockSpec(memory_space=pltpu.VMEM)
SMEM_SPEC = pl.BlockSpec(memory_space=pltpu.SMEM)


def limit(megabytes):
    return pltpu.CompilerParams(vmem_limit_bytes=megabytes * 1024 * 1024)


def kv_scratch(lanes):
    return [pltpu.VMEM((2048, lanes), BF) for _ in range(4)] + [pltpu.VMEM((2048, 256), BF) for _ in range(2)]


def cost(products):
    return pl.CostEstimate(
        flops=products * 2 * 128 * 4096 * 64, bytes_accessed=6_000_000, transcendentals=128 * 2048 * 6
    )


def attention_forward(flags, queries, keys, values):
    return pl.pallas_call(
        forward_kernel,
        out_shape=(
            jax.ShapeDtypeStruct((128, 1024), BF),
            jax.ShapeDtypeStruct((2, 960, 128), F32),
            jax.ShapeDtypeStruct((8, 1024), F32),
        ),
        in_specs=[SMEM_SPEC] + [VMEM_SPEC] * 11,
        out_specs=(VMEM_SPEC,) * 3,
        scratch_shapes=kv_scratch(128)
        + [pltpu.VMEM((2048, 384), F32) for _ in range(2)]
        + [pltpu.VMEM((2048, 384), BF) for _ in range(2)],
        compiler_params=limit(30),
        cost_estimate=cost(60),
        name="attention_forward",
    )(flags, queries, *keys, *values)


def attention_backward(flags, queries, gradient, wide, stats, tables, keys, values):
    pieces = [jax.ShapeDtypeStruct((count, 64, 640), BF) for count in (8, 8, 8, 4, 4)] * 2
    out = pl.pallas_call(
        backward_kernel,
        out_shape=tuple([jax.ShapeDtypeStruct((128, 1024), BF)] + pieces),
        in_specs=[SMEM_SPEC] + [VMEM_SPEC] * 16,
        out_specs=(VMEM_SPEC,) * 11,
        scratch_shapes=kv_scratch(128) + [pltpu.VMEM((32, 128, 128), BF) for _ in range(2)],
        compiler_params=limit(24),
        cost_estimate=cost(120),
        name="attention_backward",
    )(flags, queries, gradient, wide, stats, *tables, *keys, *values)
    return out[0], out[1:6], out[6:11]


def unpack_kernel(pack_ref, gate_ref, up_ref, down_ref, done_ref):
    def part(start):
        return pack_ref[0:15, start : start + 64, :].astype(F32).reshape(960, 640)

    gate_ref[...] = part(0)
    up_ref[...] = part(64)
    down_ref[...] = part(128)
    done_ref[...] = jnp.zeros((8, 128), F32)


def unpack_last_kernel(in_ref, out_ref, query_ref, key_ref, value_ref, gain_ref):
    out_ref[...] = in_ref[0:240, 0:960].astype(F32)
    query_ref[...] = in_ref[0:240, 960:1920].astype(F32)
    late = in_ref[:, 1920:2560].astype(F32).T
    key_ref[...] = late[0:320, 0:240]
    value_ref[...] = late[320:640, 0:240]
    gain_ref[...] = in_ref[240:256, 0:512].astype(F32)


def call(kernel, name, outs, *operands, scalars=0, room=12):
    return pl.pallas_call(
        kernel,
        out_shape=tuple(jax.ShapeDtypeStruct(shape, dtype) for shape, dtype in outs),
        in_specs=[SMEM_SPEC] * scalars + [VMEM_SPEC] * (len(operands) - scalars),
        out_specs=(VMEM_SPEC,) * len(outs),
        compiler_params=limit(room),
        name=name,
    )(*operands)


def context_scatter(keys, values, tables, later):
    block = lambda count: ((count, 64, 640), BF)
    far = ring_far(keys, values, "x", "y")
    sends = call(
        pass_on_kernel, "pass_on", (block(8),) * 4,
        keys[1], keys[2], far[0], far[1], values[1], values[2], far[2], far[3],
    )
    got = (shift(sends[0], "x", 1), shift(sends[1], "x", -1), shift(sends[2], "y", 1), shift(sends[3], "y", -1))
    moved = together(*got, *later)
    got, later = moved[:4], moved[4:]
    parts = call(far_sum_kernel, "far_sum", (block(2),) * 8, keys[0], got[0], got[1], values[0], got[2], got[3])
    near = near_scatter(parts[:4], "y") + near_scatter(parts[4:], "x")
    own, send = call(near_sum_kernel, "near_sum", (((2, 64, 640), F32), ((2, 64, 640), BF)), *near)
    return call(join_kernel, "join", (((128, 640), BF),), own, shift(send, "zh", 1), *tables)[0], *later


def weight_gradients(columns, branch, query, late, gains):
    return pl.pallas_call(
        weight_kernel,
        out_shape=jax.ShapeDtypeStruct((256, 2560), BF),
        in_specs=[VMEM_SPEC] * 17,
        out_specs=VMEM_SPEC,
        compiler_params=limit(16),
        name="weight_gradients",
    )(*columns, *branch, *query, *late, gains)


def body(
    tokens, block_pairs, w_query, key_weight, value_weight, w_out, gain_attn, gain_mlp, w_gate, w_up, w_down, cotangent
):
    rows, width = tokens.shape[1:]
    kv_width = KEY_VALUE_HEADS * HEAD_SIZE
    x_here, y_here, z_here = lax.axis_index("x"), lax.axis_index("y"), lax.axis_index("zh")
    place = 2 * lax.axis_index("zl") + lax.axis_index("co")
    context = z_here * 16 + x_here * 4 + y_here

    in_blocks = weight_blocks(jnp.concatenate([w_query, key_weight, value_weight], axis=1))
    gains = lax.all_gather(jnp.stack([gain_attn, gain_mlp])[None], FS, axis=0, tiled=True)
    gains = jnp.swapaxes(gains, 0, 1).reshape(2, width).astype(F32)
    starts = jnp.stack([place, place ^ 1, place ^ 2, place ^ 3]).astype(jnp.int32) * (width // 4)

    order = [
        ((z_here + z) % 2) * 16 + ((x_here + x + 4) % 4) * 4 + (y_here + y + 4) % 4
        for x in RING
        for y in RING
        for z in (0, 1)
    ]
    pairs = block_pairs[0][jnp.stack(order)]
    flags = jnp.where(jnp.arange(32) == 0, 1, (pairs < pairs[0]).astype(jnp.int32))
    offsets = jnp.arange(rows // 2, dtype=jnp.int32)
    query_places = jnp.concatenate(
        [pairs[0] * (rows // 2) + offsets, (63 - pairs[0]) * (rows // 2) + offsets]
    )
    frequency = 10000.0 ** (-jnp.arange(HEAD_SIZE // 2, dtype=F32) / (HEAD_SIZE // 2))
    angles = query_places.astype(F32)[:, None] * frequency[None, :]
    cosine, sine = jnp.cos(angles), jnp.sin(angles)
    cosine = jnp.concatenate([cosine] * 4, axis=1)
    sine = jnp.concatenate([-sine, sine] * 2, axis=1)
    tables = (cosine, -sine)

    weights_in, normed_low, normed_turned, flat_queries, kv = call(
        project_kernel,
        "project",
        (((width, 1600), BF), ((rows, width), BF), ((width, rows), BF), ((rows, 1024), BF), ((2, 64, 640), BF)),
        starts, tokens[0], gains, cosine, sine, *in_blocks, scalars=1, room=16,
    )
    all_keys, all_values = context_gather(kv)
    late_out, late_cotangent, own_keys = together(w_out, cotangent[0], all_keys[0])
    all_keys = (own_keys, *all_keys[1:])
    out_blocks = weight_blocks(late_out)
    upstream_blocks = pair_blocks(late_cotangent)
    attended_low, attended_wide, stats = attention_forward(flags, flat_queries, all_keys, all_values)
    out_w, middle, normed_two, attended_turned = call(
        middle_kernel,
        "middle",
        (((width, width), BF), ((rows, width), F32), ((rows, width), BF), ((width, rows), BF)),
        starts, attended_low, tokens[0], gains, *out_blocks, scalars=1,
    )
    half = ((2, rows, width), BF)
    pack, dn_near, dn_far, y_near, y_far = call(
        feed_forward_kernel,
        "feed_forward",
        (((16, 192, w_gate.shape[1]), BF), half, half, half, half),
        *pair_blocks(normed_two), *upstream_blocks, w_gate, w_up, w_down.T, room=26,
    )
    near, pack = together(add_low(dn_near, shift(dn_far, "zl", 1)), pack)
    grad_middle, grad_branch, attended_gradient, grad_gain_two = call(
        branch_kernel,
        "branch",
        (((rows, width), F32), ((rows, width), BF), ((rows, 1024), BF), ((1, width), F32)),
        near[0], shift(near[1], "co", 1), middle, gains, cotangent[0], out_w,
    )

    back = (flat_queries, attended_gradient, attended_wide, stats, tables, all_keys, all_values)
    quarter = width // 4
    pack_slots = lax.all_to_all(pack, ("x", "y"), 0, 0, tiled=True)
    columns = jnp.stack(
        [normed_turned.reshape(4, quarter, rows), attended_turned.reshape(4, quarter, rows)], axis=1
    )
    columns = column_exchange(columns, place)
    all_branch = near_blocks(grad_branch)
    grad_query_pre, key_parts, value_parts = attention_backward(flags, *back)
    far_keys, *moved = together(key_parts[3], *columns, *all_branch)
    columns, all_branch = moved[:4], moved[4:]
    key_parts = (*key_parts[:3], far_keys, key_parts[4])
    grad_query_pre = grad_query_pre[:, :width]
    back_query = right_inner(grad_query_pre, weights_in[:, :width])
    pack_slot = jnp.sum(pack_slots.astype(F32), axis=0).astype(BF)
    meanwhile = (pack_slot, shift(pack_slot, "zh", 1), back_query, *near_blocks(grad_query_pre))
    grad_kv, pack_slot, pack_other, back_query, *all_query = context_scatter(
        key_parts, value_parts, tables, meanwhile
    )
    pack_slot = add_low(pack_slot, pack_other)
    pack_all = lax.all_gather(pack_slot[None], ("x", "y"), axis=0, tiled=True)
    late = near_blocks(grad_kv)
    y_near, y_far, grad_kv = together(y_near, y_far, grad_kv)
    near = add_low(y_near, shift(y_far, "zl", 1))
    mlp_term = near[0].astype(F32) + shift(near[1], "co", 1).astype(F32)
    result = (middle + mlp_term).astype(BF)[None]
    grad_normed_one = back_query + right_inner(grad_kv, weights_in[:, width:])
    inputs = tokens[0].astype(F32)
    inverse_one = norm_forward(inputs, gains[0])[1]
    through_one, grad_gain_one = norm_backward(inputs, inverse_one, gains[0], grad_normed_one)
    input_grad = (grad_middle + through_one)[None]

    grad_gains = jnp.stack([grad_gain_one, grad_gain_two[0]]).reshape(2, 4, 1, quarter)
    gain_parts = [
        lax.dynamic_index_in_dim(grad_gains, place ^ mask, axis=1, keepdims=False) for mask in range(4)
    ]
    near_gains = jnp.stack(gain_parts[:2]) + shift(jnp.stack(gain_parts[2:]), "zl", 1)
    gains_row = (near_gains[0] + shift(near_gains[1], "co", 1)).reshape(1, 2 * quarter)
    last = weight_gradients(columns, all_branch, all_query, late, jnp.pad(gains_row, ((0, 0), (0, 512 - 2 * quarter))))
    out = slot_sum(last.reshape(16, 16, -1), ("x", "y")).astype(BF)
    out = add_low(out, shift(out, "zh", 1))
    hidden = w_gate.shape[1]
    gate_sum, up_sum, down_sum, done = call(
        unpack_kernel,
        "unpack",
        (((width, hidden), F32), ((width, hidden), F32), ((width, hidden), F32), ((8, 128), F32)),
        pack_all, room=24,
    )
    out = (out.astype(F32) + done[0, 0]).astype(BF)
    sum_last = slot_gather(out, ("x", "y")).reshape(256, -1)

    out_sum, query_sum, key_sum, value_sum, gain_sum = call(
        unpack_last_kernel,
        "unpack_last",
        (((quarter, width), F32),) * 2 + (((kv_width, quarter), F32),) * 2 + (((16, 512), F32),),
        sum_last, room=16,
    )
    return (
        result,
        input_grad,
        query_sum,
        key_sum.T,
        value_sum.T,
        out_sum,
        gain_sum[0, :quarter],
        gain_sum[0, quarter : 2 * quarter],
        gate_sum,
        up_sum,
        down_sum.T,
    )


def solution(mesh):
    split = Mesh(mesh.devices.reshape(2, 4, 4, 2, 2), ("zh", "x", "y", "zl", "co"))
    ctx = ("zh", "x", "y")
    in_specs = (
        P(FS, ctx, None),
        P(FS, None),
        P(FS, None),
        P(FS, None),
        P(FS, None),
        P(FS, None),
        P(FS),
        P(FS),
        P(None, FS),
        P(None, FS),
        P(FS, None),
        P(FS, ctx, None),
    )
    out_specs = (
        P(FS, ctx, None),
        P(FS, ctx, None),
        P(FS, None),
        P(FS, None),
        P(FS, None),
        P(FS, None),
        P(FS),
        P(FS),
        P(None, FS),
        P(None, FS),
        P(FS, None),
    )
    return jax.shard_map(body, mesh=split, in_specs=in_specs, out_specs=out_specs, check_vma=False)
```

```python
import functools

import jax
import jax.numpy as jnp
from jax import lax
from jax.experimental import pallas as pl
from jax.experimental.pallas import tpu as pltpu
from jax.sharding import Mesh, PartitionSpec as P

QUERY_HEADS = 15
KEY_VALUE_HEADS = 5
HEAD_SIZE = 64
EPSILON = 1e-05
BF = jnp.bfloat16
F32 = jnp.float32
FS = ("zl", "co")
RING = (0, -1, 1, 2)


def matrix_product(left, right):
    return jnp.dot(left, right, preferred_element_type=F32)


def left_inner(left, right):
    return lax.dot_general(left, right, (((0,), (0,)), ((), ())), preferred_element_type=F32)


def right_inner(left, right):
    return lax.dot_general(left, right, (((1,), (1,)), ((), ())), preferred_element_type=F32)


def shift(value, axis, step):
    count = lax.axis_size(axis)
    return lax.ppermute(value, axis, [(i, (i + step) % count) for i in range(count)])


def add_low(*parts):
    total = parts[0].astype(F32)
    for part in parts[1:]:
        total = total + part.astype(F32)
    return total.astype(BF)


def together(*values):
    return lax.optimization_barrier(values)


def ring_pick(value, axis):
    here = lax.axis_index(axis)
    return [
        lax.dynamic_index_in_dim(value, lax.rem(here + off + 4, 4), axis=0, keepdims=False) for off in RING
    ]


def ring_place(blocks, axis):
    here = lax.axis_index(axis)
    out = jnp.stack(blocks)
    for block, off in zip(blocks, RING):
        out = lax.dynamic_update_slice_in_dim(out, block[None], lax.rem(here + off + 4, 4), axis=0)
    return out


def near_gather(value, axis):
    return [value, shift(value, axis, 1), shift(value, axis, -1), shift(value, axis, 2)]


def near_scatter(blocks, axis):
    return [blocks[0], shift(blocks[1], axis, -1), shift(blocks[2], axis, 1), shift(blocks[3], axis, 2)]


def two_ring_gather(one, two, axis_one, axis_two):
    left_one, right_one, left_two, right_two = (
        shift(one, axis_one, 1), shift(one, axis_one, -1), shift(two, axis_two, 1), shift(two, axis_two, -1)
    )
    half = one.shape[0] // 2
    far = (
        shift(left_one[:half], axis_one, 1),
        shift(right_one[half:], axis_one, -1),
        shift(left_two[:half], axis_two, 1),
        shift(right_two[half:], axis_two, -1),
    )
    return (one, left_one, right_one, far[0], far[1]), (two, left_two, right_two, far[2], far[3])


def ring_far(one, two, axis_one, axis_two):
    return (
        shift(one[3], axis_one, 1), shift(one[4], axis_one, -1), shift(two[3], axis_two, 1), shift(two[4], axis_two, -1)
    )


def pair_gather(value):
    both = jnp.concatenate([value[None], shift(value, "zl", 1)[None]], axis=0)
    other = shift(both, "co", 1)
    return jnp.stack([both[0], other[0], both[1], other[1]])


def pair_blocks(value):
    far = shift(value, "zl", 1)
    return value, shift(value, "co", 1), far, shift(far, "co", 1)


def near_blocks(value):
    return tuple(lax.ppermute(value, FS, [(i, i ^ mask) for i in range(4)]) if mask else value for mask in range(4))


def pair_scatter(value):
    near = add_low(value[:2], shift(value[2:].astype(BF), "zl", 1))
    return near[0].astype(F32) + shift(near[1], "co", 1).astype(F32)


def weight_blocks(value):
    cut = 128
    zed = ("zh", "zl")
    one = shift(value[:cut], zed, 1)
    two = shift(value[cut:], zed, -1)
    return value, shift(value, "co", 1), one, two, shift(one, "co", 1), shift(two, "co", 1)


def context_gather(both):
    other = shift(both, "zh", 1)
    keys = jnp.concatenate(near_gather(jnp.stack([both[0], other[0]]), "y"))
    values = jnp.concatenate(near_gather(jnp.stack([both[1], other[1]]), "x"))
    return two_ring_gather(keys, values, "x", "y")


def slot_sum(value, axes):
    parts = lax.all_to_all(value, axes, 0, 0, tiled=True)
    return jnp.sum(parts.astype(F32), axis=0)


def slot_gather(value, axes):
    count = lax.axis_size(axes)
    return lax.all_to_all(jnp.broadcast_to(value[None], (count,) + value.shape), axes, 0, 0, tiled=True)


def column_exchange(value, place):
    parts = []
    for mask in range(4):
        part = lax.dynamic_index_in_dim(value, place ^ mask, axis=0, keepdims=False)
        parts.append(lax.ppermute(part, FS, [(i, i ^ mask) for i in range(4)]) if mask else part)
    return parts


def apply_rotation(values, cosine_table, sinusoid_table):
    half = values.shape[-1] // 2
    leading, trailing = values[..., :half], values[..., half:]
    return jnp.concatenate(
        [
            leading * cosine_table - trailing * sinusoid_table,
            trailing * cosine_table + leading * sinusoid_table,
        ],
        axis=-1,
    )


def norm_forward(values, gain_vector):
    inverse = lax.rsqrt(jnp.mean(values * values, axis=-1, keepdims=True) + EPSILON)
    return (values * inverse * gain_vector, inverse)


def norm_backward(values, inverse, gain_vector, gradient):
    weighted = gradient * gain_vector
    through = inverse * weighted - values * inverse**3 * jnp.mean(
        weighted * values, axis=-1, keepdims=True
    )
    return (through, jnp.sum(gradient * values * inverse, axis=0))


HEAD_GROUPS = ((0, 2), (1, 2), (2, 1))
NEGATIVE = -1e30


def nt(left, right):
    return lax.dot_general(left, right, (((1,), (1,)), ((), ())), preferred_element_type=F32)


def tn(left, right):
    return lax.dot_general(left, right, (((0,), (0,)), ((), ())), preferred_element_type=F32)


def swap_halves(slab):
    return jnp.concatenate([slab[:, 64:], slab[:, :64]], axis=1)


def spread_heads(rows, kv_heads):
    lane = lax.broadcasted_iota(jnp.int32, (64, 128), 1)
    blocks = []
    for kv in range(kv_heads):
        for group in range(3):
            head = 3 * kv + group
            slab = rows[:, 128 * (head // 2) : 128 * (head // 2) + 128]
            if head % 2 != kv:
                slab = swap_halves(slab)
            blocks.append(jnp.where((lane < 64) == (kv == 0), slab, 0.0))
    return jnp.concatenate(blocks, axis=0)


def unspread_heads(blocks, kv_heads):
    lane = lax.broadcasted_iota(jnp.int32, (64, 128), 1)
    count = 3 * kv_heads
    slabs = []
    for slab in range((count + 1) // 2):
        halves = []
        for side in range(2):
            head = 2 * slab + side
            if head >= count:
                halves.append(jnp.zeros((64, 128), F32))
                continue
            block = blocks[64 * head : 64 * head + 64]
            halves.append(block if head // 3 == side else swap_halves(block))
        slabs.append(jnp.where(lane < 64, halves[0], halves[1]))
    return jnp.concatenate(slabs, axis=1)


def causal_mask(columns):
    key = lax.broadcasted_iota(jnp.int32, (64, columns), 0)
    query = lax.rem(lax.broadcasted_iota(jnp.int32, (64, columns), 1), 64)
    return key <= query


def fill_chunks(pieces, low, high, outer_first, index, width):
    if width % 128:
        zeros = jnp.zeros((2048, 64), BF)
        low[:, width : width + 64] = zeros
        high[:, width : width + 64] = zeros
    start = 256 * index
    for chunk in range(32):
        one, two, zed = chunk // 8, (chunk // 2) % 4, chunk % 2
        outer, inner = (one, two) if outer_first else (two, one)
        if outer < 3:
            block = pieces[outer].at[2 * inner + zed]
        else:
            block = pieces[3 + inner // 2].at[2 * (inner % 2) + zed]
        low[64 * chunk : 64 * chunk + 64, 0:width] = block[:, start : start + width]
        high[64 * chunk : 64 * chunk + 64, 0:width] = block[:, start + width : start + 2 * width]


def blocks_beside(value):
    low, high = value[0:64], value[64:128]
    return jnp.concatenate(
        [low[:, 0:128], high[:, 0:128], low[:, 128:256], high[:, 128:256], low[:, 256:320], high[:, 256:320]], axis=1
    )


def blocks_apart(value):
    low = jnp.concatenate([value[:, 0:128], value[:, 256:384], value[:, 512:640]], axis=1)
    high = jnp.concatenate([value[:, 128:256], value[:, 384:512], swap_halves(value[:, 512:640])], axis=1)
    return jnp.concatenate([low, high], axis=0)


def mix_chunks(flags, low, high, mixed, lanes):
    def step(chunk, carry):
        rows = pl.ds(pl.multiple_of(chunk * 64, 64), 64)
        chosen = flags[chunk] > 0
        mixed[rows, 0:128] = jnp.where(chosen, low[rows, lanes], jnp.zeros((64, 128), BF))
        mixed[rows, 128:256] = jnp.where(chosen, jnp.zeros((64, 128), BF), high[rows, lanes])
        return carry

    lax.fori_loop(0, 32, step, 0)


def fold_rows(value, op):
    parts = value.reshape(value.shape[0] // 8, 8, value.shape[1])
    return op(parts, axis=0)


def forward_kernel(flags, q_ref, k0, k1, k2, k3, k4, v0, v1, v2, v3, v4, att_ref, wide_ref, stat_ref,
                   k_low, k_high, v_low, v_high, k_mix, v_mix, s_one, s_two, p_one, p_two):
    stat_ref[...] = jnp.zeros(stat_ref.shape, F32)
    lanes = slice(0, 128)
    for index, kv_heads in HEAD_GROUPS:
        fill_chunks((k0, k1, k2, k3, k4), k_low, k_high, True, index, 64 * kv_heads)
        fill_chunks((v0, v1, v2, v3, v4), v_low, v_high, False, index, 64 * kv_heads)
        n = 192 * kv_heads
        wide = 128 * ((3 * kv_heads + 1) // 2)
        columns = slice(384 * index, 384 * index + wide)
        q_all = q_ref[:, columns].astype(F32) * 0.125
        q_low = spread_heads(q_all[0:64], kv_heads).astype(BF)
        q_high = spread_heads(q_all[64:128], kv_heads).astype(BF)
        q_both = jnp.concatenate([q_low, q_high], axis=1)
        mix_chunks(flags, k_low, k_high, k_mix, lanes)
        mix_chunks(flags, v_low, v_high, v_mix, lanes)
        allowed = causal_mask(n)
        tail = jnp.where(allowed, nt(k_high[0:64, lanes], q_high), NEGATIVE)
        floor = jnp.full((8, n), NEGATIVE, F32)

        def scores(block, carry):
            max_low, max_high = carry
            rows = pl.ds(pl.multiple_of(block * 256, 256), 256)
            one = nt(k_low[rows, lanes], q_high)
            s_one[rows, 0:n] = one
            max_high = jnp.maximum(max_high, fold_rows(one, jnp.max))
            two = nt(k_mix[rows, :], q_both)
            first = jnp.where(jnp.logical_or(allowed, block > 0), two[0:64], NEGATIVE)
            two = jnp.concatenate([first, two[64:]], axis=0)
            s_two[rows, 0:n] = two
            for part in range(4):
                top = fold_rows(two[64 * part : 64 * part + 64], jnp.max)
                chosen = flags[block * 4 + part] > 0
                max_low = jnp.maximum(max_low, jnp.where(chosen, top, NEGATIVE))
                max_high = jnp.maximum(max_high, jnp.where(chosen, NEGATIVE, top))
            return max_low, max_high

        max_low, max_high = lax.fori_loop(0, 8, scores, (floor, fold_rows(tail, jnp.max)))
        max_low = jnp.max(max_low, axis=0, keepdims=True)
        max_high = jnp.max(max_high, axis=0, keepdims=True)
        tail = jnp.exp(tail - max_high)

        def weights(block, carry):
            sum_low, sum_high = carry
            rows = pl.ds(pl.multiple_of(block * 256, 256), 256)
            one = jnp.exp(s_one[rows, 0:n] - max_high)
            p_one[rows, 0:n] = one.astype(BF)
            sum_high = sum_high + fold_rows(one, jnp.sum)
            for part in range(4):
                chosen = flags[block * 4 + part] > 0
                small = pl.ds(pl.multiple_of(block * 256 + 64 * part, 64), 64)
                two = jnp.exp(s_two[small, 0:n] - jnp.where(chosen, max_low, max_high))
                p_two[small, 0:n] = two.astype(BF)
                total = fold_rows(two, jnp.sum)
                sum_low = sum_low + jnp.where(chosen, total, 0.0)
                sum_high = sum_high + jnp.where(chosen, 0.0, total)
            return sum_low, sum_high

        sum_low, sum_high = lax.fori_loop(
            0, 8, weights, (jnp.zeros((8, n), F32), fold_rows(tail, jnp.sum))
        )
        sum_low = jnp.sum(sum_low, axis=0, keepdims=True)
        sum_high = jnp.sum(sum_high, axis=0, keepdims=True)
        out_two = tn(v_mix[...], p_two[:, 0:n])
        out_high = tn(v_low[:, lanes], p_one[:, 0:n]) + out_two[128:256]
        out_high = (out_high + tn(v_high[0:64, lanes], tail.astype(BF))) / sum_high
        out_low = out_two[0:128] / sum_low
        out_low, out_high = out_low.T, out_high.T
        span = slice(384 * index, 384 * index + n)
        wide_ref[0, span, :] = out_low
        wide_ref[1, span, :] = out_high
        att_ref[0:64, columns] = unspread_heads(out_low, kv_heads).astype(BF)
        att_ref[64:128, columns] = unspread_heads(out_high, kv_heads).astype(BF)
        stat_ref[0:1, span] = max_low + jnp.log(sum_low)
        stat_ref[1:2, span] = max_high + jnp.log(sum_high)


def rotate_slabs(value, cosine, sine):
    lane = lax.broadcasted_iota(jnp.int32, (value.shape[0], 128), 1)
    slabs = []
    for start in range(0, value.shape[1], 128):
        slab = value[:, start : start + 128]
        other = jnp.where(lane % 64 < 32, pltpu.roll(slab, 96, 1), pltpu.roll(slab, 32, 1))
        slabs.append(slab * cosine + other * sine)
    return jnp.concatenate(slabs, axis=1)


def backward_kernel(flags, q_ref, d_ref, wide_ref, stat_ref, cos_ref, sin_ref,
                    k0, k1, k2, k3, k4, v0, v1, v2, v3, v4,
                    dq_ref, dk0, dk1, dk2, dk3, dk4, dv0, dv1, dv2, dv3, dv4,
                    k_low, k_high, v_low, v_high, k_mix, v_mix, dk_all, dv_all):
    for index, kv_heads in HEAD_GROUPS:
        fill_chunks((k0, k1, k2, k3, k4), k_low, k_high, True, index, 64 * kv_heads)
        fill_chunks((v0, v1, v2, v3, v4), v_low, v_high, False, index, 64 * kv_heads)
        lanes = slice(0, 128)
        n = 192 * kv_heads
        wide = 128 * ((3 * kv_heads + 1) // 2)
        columns = slice(384 * index, 384 * index + wide)
        span = slice(384 * index, 384 * index + n)
        q_all = q_ref[:, columns].astype(F32) * 0.125
        d_all = d_ref[:, columns].astype(F32)
        q_low = spread_heads(q_all[0:64], kv_heads).astype(BF)
        q_high = spread_heads(q_all[64:128], kv_heads).astype(BF)
        q_both = jnp.concatenate([q_low, q_high], axis=1)
        d_low = spread_heads(d_all[0:64], kv_heads)
        d_high = spread_heads(d_all[64:128], kv_heads)
        ones = jnp.ones((8, 128), F32)

        def row_sums(value):
            return lax.dot_general(
                ones, value, (((1,), (1,)), ((), ())),
                precision=lax.Precision.HIGHEST, preferred_element_type=F32,
            )[0:1]

        delta_low = row_sums(d_low * wide_ref[0, span, :])
        delta_high = row_sums(d_high * wide_ref[1, span, :])
        d_low, d_high = d_low.astype(BF), d_high.astype(BF)
        d_both = jnp.concatenate([d_low, d_high], axis=1)
        log_low, log_high = stat_ref[0:1, span], stat_ref[1:2, span]
        mix_chunks(flags, k_low, k_high, k_mix, lanes)
        mix_chunks(flags, v_low, v_high, v_mix, lanes)
        allowed = causal_mask(n)

        own_k, own_v = k_high[0:64, lanes], v_high[0:64, lanes]
        soft = jnp.where(allowed, jnp.exp(nt(own_k, q_high) - log_high), 0.0)
        grad = (soft * (nt(own_v, d_high) - delta_high)).astype(BF)
        tail_k = matrix_product(grad, q_high)
        tail_v = matrix_product(soft.astype(BF), d_high)
        start_high = tn(own_k, grad)

        def step(block, carry):
            dq_low, dq_high = carry
            rows = pl.ds(pl.multiple_of(block * 256, 256), 256)
            k_one, v_one = k_low[rows, lanes], v_low[rows, lanes]
            soft = jnp.exp(nt(k_one, q_high) - log_high)
            grad = (soft * (nt(v_one, d_high) - delta_high)).astype(BF)
            dk_one = matrix_product(grad, q_high)
            dv_one = matrix_product(soft.astype(BF), d_high)
            dq_high = dq_high + tn(k_one, grad)
            k_two, v_two = k_mix[rows, :], v_mix[rows, :]
            two = nt(k_two, q_both)
            two_grad = nt(v_two, d_both)
            softs, grads = [], []
            for part in range(4):
                chosen = flags[block * 4 + part] > 0
                inner = slice(64 * part, 64 * part + 64)
                soft = jnp.exp(two[inner] - jnp.where(chosen, log_low, log_high))
                if part == 0:
                    soft = jnp.where(jnp.logical_or(allowed, block > 0), soft, 0.0)
                softs.append(soft.astype(BF))
                grads.append(
                    (soft * (two_grad[inner] - jnp.where(chosen, delta_low, delta_high))).astype(BF)
                )
            soft = jnp.concatenate(softs, axis=0)
            grad = jnp.concatenate(grads, axis=0)
            dk_two = matrix_product(grad, q_both)
            dv_two = matrix_product(soft, d_both)
            both = tn(k_two, grad)
            for part in range(4):
                chosen = flags[block * 4 + part] > 0
                inner = slice(64 * part, 64 * part + 64)
                chunk = block * 4 + part
                for one, other, out in ((dk_one, dk_two, dk_all), (dv_one, dv_two, dv_all)):
                    out[chunk, 0:64, :] = (one[inner] + jnp.where(chosen, other[inner, 0:128], 0.0)).astype(BF)
                    out[chunk, 64:128, :] = jnp.where(chosen, 0.0, other[inner, 128:256]).astype(BF)
            return dq_low + both[0:128], dq_high + both[128:256]

        dq_low, dq_high = lax.fori_loop(0, 8, step, (jnp.zeros((128, n), F32), start_high))
        dk_all[0, 64:128, :] = tail_k.astype(BF)
        dv_all[0, 64:128, :] = tail_v.astype(BF)
        width, start = 64 * kv_heads, 256 * index
        for pieces, whole, outer_first in (
            ((dk0, dk1, dk2, dk3, dk4), dk_all, True),
            ((dv0, dv1, dv2, dv3, dv4), dv_all, False),
        ):
            for chunk in range(32):
                one, two, zed = chunk // 8, (chunk // 2) % 4, chunk % 2
                outer, inner = (one, two) if outer_first else (two, one)
                if outer < 3:
                    piece, spot = pieces[outer], 2 * inner + zed
                else:
                    piece, spot = pieces[3 + inner // 2], 2 * (inner % 2) + zed
                piece[spot, :, start : start + width] = whole[chunk, 0:64, 0:width]
                piece[spot, :, start + width : start + 2 * width] = whole[chunk, 64:128, 0:width]
        for start, part in ((0, dq_low), (64, dq_high)):
            here = slice(start, start + 64)
            part = unspread_heads(part.T, kv_heads) * 0.125
            dq_ref[here, columns] = rotate_slabs(part, cos_ref[here, :], sin_ref[here, :]).astype(BF)


def place_rows(out_ref, starts, blocks):
    own, core, one, two, core_one, core_two = blocks
    for place, block, first, count in (
        (0, own, 0, 240),
        (1, core, 0, 240),
        (2, one, 0, 128),
        (2, two, 128, 112),
        (3, core_one, 0, 128),
        (3, core_two, 128, 112),
    ):
        rows = pl.ds(pl.multiple_of(starts[place] + first, 16), count)
        out_ref[rows, :] = block[...]


def project_kernel(starts, x_ref, gain_ref, cos_ref, sin_ref, b0, b1, b2, b3, b4, b5,
                   w_ref, n_ref, nt_ref, q_ref, kv_ref):
    place_rows(w_ref, starts, (b0, b1, b2, b3, b4, b5))
    x = x_ref[...].astype(F32)
    normed, _ = norm_forward(x, gain_ref[0:1, :])
    low = normed.astype(BF)
    n_ref[...] = low
    nt_ref[...] = low.astype(F32).T.astype(BF)
    product = matrix_product(low, w_ref[...])
    turned = rotate_slabs(product[:, 0:1280], cos_ref[...], sin_ref[...])
    q_ref[:, 0:960] = turned[:, 0:960].astype(BF)
    q_ref[:, 960:1024] = jnp.zeros((128, 64), BF)
    kv_ref[0] = blocks_beside(turned[:, 960:1280]).astype(BF)
    kv_ref[1] = blocks_beside(product[:, 1280:1600]).astype(BF)


def middle_kernel(starts, att_ref, x_ref, gain_ref, b0, b1, b2, b3, b4, b5, w_ref, mid_ref, n_ref, at_ref):
    place_rows(w_ref, starts, (b0, b1, b2, b3, b4, b5))
    low = att_ref[:, 0:960]
    at_ref[...] = low.astype(F32).T.astype(BF)
    middle = x_ref[...].astype(F32) + matrix_product(low, w_ref[...])
    mid_ref[...] = middle
    n_ref[...] = norm_forward(middle, gain_ref[1:2, :])[0].astype(BF)


def feed_forward_kernel(n0, n1, n2, n3, c0, c1, c2, c3, wg_ref, wu_ref, wd_ref,
                        pack_ref, dn_near, dn_far, y_near, y_far):
    normed = jnp.concatenate([n0[...], n1[...], n2[...], n3[...]], axis=0)
    upstream = jnp.concatenate([c0[...], c1[...], c2[...], c3[...]], axis=0)
    gate = matrix_product(normed, wg_ref[...])
    up = matrix_product(normed, wu_ref[...])
    grad_hidden = matrix_product(upstream, wd_ref[...])
    sigmoid = 1.0 / (1.0 + jnp.exp(-gate))
    silu = gate * sigmoid
    hidden = (silu * up).astype(BF)
    grad_up = (grad_hidden * silu).astype(BF)
    grad_gate = (grad_hidden * up * sigmoid * (1.0 + gate * (1.0 - sigmoid))).astype(BF)
    back = (nt(grad_gate, wg_ref[...]) + nt(grad_up, wu_ref[...])).astype(BF)
    dn_near[...] = back[0:256].reshape(2, 128, 960)
    dn_far[...] = back[256:512].reshape(2, 128, 960)
    result = nt(hidden, wd_ref[...]).astype(BF)
    y_near[...] = result[0:256].reshape(2, 128, 960)
    y_far[...] = result[256:512].reshape(2, 128, 960)
    for start, left, right in ((0, normed, grad_gate), (64, normed, grad_up), (128, upstream, hidden)):
        pack_ref[0:15, start : start + 64, :] = tn(left, right).astype(BF).reshape(15, 64, 640)
    pack_ref[15] = jnp.zeros((192, 640), BF)


def branch_kernel(own_ref, core_ref, mid_ref, gain_ref, cot_ref, w_ref, grad_ref, low_ref, d_ref, gain_out):
    d_normed = own_ref[...].astype(F32) + core_ref[...].astype(F32)
    middle = mid_ref[...]
    gain = gain_ref[1:2, :]
    inverse = lax.rsqrt(jnp.mean(middle * middle, axis=-1, keepdims=True) + EPSILON)
    weighted = d_normed * gain
    through = inverse * weighted - middle * inverse**3 * jnp.mean(weighted * middle, axis=-1, keepdims=True)
    gain_out[...] = jnp.sum(d_normed * middle * inverse, axis=0, keepdims=True)
    grad = cot_ref[...].astype(F32) + through
    grad_ref[...] = grad
    low = grad.astype(BF)
    low_ref[...] = low
    d_ref[:, 0:960] = nt(low, w_ref[...]).astype(BF)
    d_ref[:, 960:1024] = jnp.zeros((128, 64), BF)


def pass_on_kernel(*refs):
    for pair in range(2):
        left, right, from_left, from_right = refs[4 * pair : 4 * pair + 4]
        send_right, send_left = refs[8 + 2 * pair : 10 + 2 * pair]
        for chunk in range(8):
            if chunk < 4:
                send_right[chunk] = (right[chunk].astype(F32) + from_left[chunk].astype(F32)).astype(BF)
                send_left[chunk] = left[chunk]
            else:
                send_right[chunk] = right[chunk]
                send_left[chunk] = (left[chunk].astype(F32) + from_right[chunk - 4].astype(F32)).astype(BF)


def far_sum_kernel(*refs):
    for pair in range(2):
        own, one, two = refs[3 * pair : 3 * pair + 3]
        outs = refs[6 + 4 * pair : 10 + 4 * pair]
        for chunk in range(8):
            total = own[chunk].astype(F32) + one[chunk].astype(F32) + two[chunk].astype(F32)
            outs[chunk // 2][chunk % 2] = total.astype(BF)


def near_sum_kernel(*refs):
    own_ref, send_ref = refs[8:]
    for pair in range(2):
        total = refs[4 * pair][...].astype(F32)
        for part in refs[4 * pair + 1 : 4 * pair + 4]:
            total = total + part[...].astype(F32)
        own_ref[pair] = total[0]
        send_ref[pair] = total[1].astype(BF)


def join_kernel(own_ref, other_ref, cos_ref, sin_ref, out_ref):
    total = own_ref[...] + other_ref[...].astype(F32)
    keys = rotate_slabs(blocks_apart(total[0]), cos_ref[...], sin_ref[...])
    out_ref[:, 0:320] = keys[:, 0:320].astype(BF)
    out_ref[:, 320:640] = blocks_apart(total[1])[:, 0:320].astype(BF)


def weight_kernel(c0, c1, c2, c3, b0, b1, b2, b3, e0, e1, e2, e3, g0, g1, g2, g3, gains_ref, out_ref):
    columns = [jnp.concatenate([c[place] for c in (c0, c1, c2, c3)], axis=1) for place in range(2)]
    branch = jnp.concatenate([b0[...], b1[...], b2[...], b3[...]], axis=0)
    query = jnp.concatenate([e0[...], e1[...], e2[...], e3[...]], axis=0)
    late = jnp.concatenate([g0[...], g1[...], g2[...], g3[...]], axis=0)
    out_ref[0:240, 0:960] = matrix_product(columns[1], branch).astype(BF)
    out_ref[0:240, 960:1920] = matrix_product(columns[0], query).astype(BF)
    out_ref[0:240, 1920:2560] = matrix_product(columns[0], late).astype(BF)
    out_ref[240:256, :] = jnp.zeros((16, 2560), BF)
    row = lax.broadcasted_iota(jnp.int32, (16, 512), 0)
    out_ref[240:256, 0:512] = jnp.where(row == 0, jnp.broadcast_to(gains_ref[0:1, :], (16, 512)), 0.0).astype(BF)


VMEM_SPEC = pl.BlockSpec(memory_space=pltpu.VMEM)
SMEM_SPEC = pl.BlockSpec(memory_space=pltpu.SMEM)


def limit(megabytes):
    return pltpu.CompilerParams(vmem_limit_bytes=megabytes * 1024 * 1024)


def kv_scratch(lanes):
    return [pltpu.VMEM((2048, lanes), BF) for _ in range(4)] + [pltpu.VMEM((2048, 256), BF) for _ in range(2)]


def cost(products):
    return pl.CostEstimate(
        flops=products * 2 * 128 * 4096 * 64, bytes_accessed=6_000_000, transcendentals=128 * 2048 * 6
    )


def attention_forward(flags, queries, keys, values):
    return pl.pallas_call(
        forward_kernel,
        out_shape=(
            jax.ShapeDtypeStruct((128, 1024), BF),
            jax.ShapeDtypeStruct((2, 960, 128), F32),
            jax.ShapeDtypeStruct((8, 1024), F32),
        ),
        in_specs=[SMEM_SPEC] + [VMEM_SPEC] * 11,
        out_specs=(VMEM_SPEC,) * 3,
        scratch_shapes=kv_scratch(128)
        + [pltpu.VMEM((2048, 384), F32) for _ in range(2)]
        + [pltpu.VMEM((2048, 384), BF) for _ in range(2)],
        compiler_params=limit(30),
        cost_estimate=cost(60),
        name="attention_forward",
    )(flags, queries, *keys, *values)


def attention_backward(flags, queries, gradient, wide, stats, tables, keys, values):
    pieces = [jax.ShapeDtypeStruct((count, 64, 640), BF) for count in (8, 8, 8, 4, 4)] * 2
    out = pl.pallas_call(
        backward_kernel,
        out_shape=tuple([jax.ShapeDtypeStruct((128, 1024), BF)] + pieces),
        in_specs=[SMEM_SPEC] + [VMEM_SPEC] * 16,
        out_specs=(VMEM_SPEC,) * 11,
        scratch_shapes=kv_scratch(128) + [pltpu.VMEM((32, 128, 128), BF) for _ in range(2)],
        compiler_params=limit(24),
        cost_estimate=cost(120),
        name="attention_backward",
    )(flags, queries, gradient, wide, stats, *tables, *keys, *values)
    return out[0], out[1:6], out[6:11]


def unpack_kernel(pack_ref, gate_ref, up_ref, down_ref, done_ref):
    def part(start):
        return pack_ref[0:15, start : start + 64, :].astype(F32).reshape(960, 640)

    gate_ref[...] = part(0)
    up_ref[...] = part(64)
    down_ref[...] = part(128)
    done_ref[...] = jnp.zeros((8, 128), F32)


def unpack_last_kernel(in_ref, _, out_ref, query_ref, key_ref, value_ref, gain_ref):
    out_ref[...] = in_ref[0:240, 0:960].astype(F32)
    query_ref[...] = in_ref[0:240, 960:1920].astype(F32)
    late = in_ref[:, 1920:2560].astype(F32).T
    key_ref[...] = late[0:320, 0:240]
    value_ref[...] = late[320:640, 0:240]
    gain_ref[...] = in_ref[240:256, 0:512].astype(F32)


def call(kernel, name, outs, *operands, scalars=0, room=12):
    return pl.pallas_call(
        kernel,
        out_shape=tuple(jax.ShapeDtypeStruct(shape, dtype) for shape, dtype in outs),
        in_specs=[SMEM_SPEC] * scalars + [VMEM_SPEC] * (len(operands) - scalars),
        out_specs=(VMEM_SPEC,) * len(outs),
        compiler_params=limit(room),
        name=name,
    )(*operands)


def context_scatter(keys, values, tables, later):
    block = lambda count: ((count, 64, 640), BF)
    far = ring_far(keys, values, "x", "y")
    sends = call(
        pass_on_kernel, "pass_on", (block(8),) * 4,
        keys[1], keys[2], far[0], far[1], values[1], values[2], far[2], far[3],
    )
    got = (shift(sends[0], "x", 1), shift(sends[1], "x", -1), shift(sends[2], "y", 1), shift(sends[3], "y", -1))
    moved = together(*got, *later)
    got, later = moved[:4], moved[4:]
    parts = call(far_sum_kernel, "far_sum", (block(2),) * 8, keys[0], got[0], got[1], values[0], got[2], got[3])
    near = near_scatter(parts[:4], "y") + near_scatter(parts[4:], "x")
    own, send = call(near_sum_kernel, "near_sum", (((2, 64, 640), F32), ((2, 64, 640), BF)), *near)
    return call(join_kernel, "join", (((128, 640), BF),), own, shift(send, "zh", 1), *tables)[0], *later


def weight_gradients(columns, branch, query, late, gains):
    return pl.pallas_call(
        weight_kernel,
        out_shape=jax.ShapeDtypeStruct((256, 2560), BF),
        in_specs=[VMEM_SPEC] * 17,
        out_specs=VMEM_SPEC,
        compiler_params=limit(16),
        name="weight_gradients",
    )(*columns, *branch, *query, *late, gains)


def body(
    tokens, block_pairs, w_query, key_weight, value_weight, w_out, gain_attn, gain_mlp, w_gate, w_up, w_down, cotangent
):
    rows, width = tokens.shape[1:]
    kv_width = KEY_VALUE_HEADS * HEAD_SIZE
    x_here, y_here, z_here = lax.axis_index("x"), lax.axis_index("y"), lax.axis_index("zh")
    place = 2 * lax.axis_index("zl") + lax.axis_index("co")
    context = z_here * 16 + x_here * 4 + y_here

    in_blocks = weight_blocks(jnp.concatenate([w_query, key_weight, value_weight], axis=1))
    gains = lax.all_gather(jnp.stack([gain_attn, gain_mlp])[None], FS, axis=0, tiled=True)
    gains = jnp.swapaxes(gains, 0, 1).reshape(2, width).astype(F32)
    starts = jnp.stack([place, place ^ 1, place ^ 2, place ^ 3]).astype(jnp.int32) * (width // 4)

    order = [
        ((z_here + z) % 2) * 16 + ((x_here + x + 4) % 4) * 4 + (y_here + y + 4) % 4
        for x in RING
        for y in RING
        for z in (0, 1)
    ]
    pairs = block_pairs[0][jnp.stack(order)]
    flags = jnp.where(jnp.arange(32) == 0, 1, (pairs < pairs[0]).astype(jnp.int32))
    offsets = jnp.arange(rows // 2, dtype=jnp.int32)
    query_places = jnp.concatenate(
        [pairs[0] * (rows // 2) + offsets, (63 - pairs[0]) * (rows // 2) + offsets]
    )
    frequency = 10000.0 ** (-jnp.arange(HEAD_SIZE // 2, dtype=F32) / (HEAD_SIZE // 2))
    angles = query_places.astype(F32)[:, None] * frequency[None, :]
    cosine, sine = jnp.cos(angles), jnp.sin(angles)
    cosine = jnp.concatenate([cosine] * 4, axis=1)
    sine = jnp.concatenate([-sine, sine] * 2, axis=1)
    tables = (cosine, -sine)

    weights_in, normed_low, normed_turned, flat_queries, kv = call(
        project_kernel,
        "project",
        (((width, 1600), BF), ((rows, width), BF), ((width, rows), BF), ((rows, 1024), BF), ((2, 64, 640), BF)),
        starts, tokens[0], gains, cosine, sine, *in_blocks, scalars=1, room=16,
    )
    all_keys, all_values = context_gather(kv)
    late_out, late_cotangent, own_keys = together(w_out, cotangent[0], all_keys[0])
    all_keys = (own_keys, *all_keys[1:])
    out_blocks = weight_blocks(late_out)
    upstream_blocks = pair_blocks(late_cotangent)
    attended_low, attended_wide, stats = attention_forward(flags, flat_queries, all_keys, all_values)
    out_w, middle, normed_two, attended_turned = call(
        middle_kernel,
        "middle",
        (((width, width), BF), ((rows, width), F32), ((rows, width), BF), ((width, rows), BF)),
        starts, attended_low, tokens[0], gains, *out_blocks, scalars=1,
    )
    half = ((2, rows, width), BF)
    pack, dn_near, dn_far, y_near, y_far = call(
        feed_forward_kernel,
        "feed_forward",
        (((16, 192, w_gate.shape[1]), BF), half, half, half, half),
        *pair_blocks(normed_two), *upstream_blocks, w_gate, w_up, w_down.T, room=26,
    )
    near, pack = together(add_low(dn_near, shift(dn_far, "zl", 1)), pack)
    grad_middle, grad_branch, attended_gradient, grad_gain_two = call(
        branch_kernel,
        "branch",
        (((rows, width), F32), ((rows, width), BF), ((rows, 1024), BF), ((1, width), F32)),
        near[0], shift(near[1], "co", 1), middle, gains, cotangent[0], out_w,
    )

    back = (flat_queries, attended_gradient, attended_wide, stats, tables, all_keys, all_values)
    quarter = width // 4
    pack_slots = lax.all_to_all(pack, ("x", "y"), 0, 0, tiled=True)
    columns = jnp.stack(
        [normed_turned.reshape(4, quarter, rows), attended_turned.reshape(4, quarter, rows)], axis=1
    )
    columns = column_exchange(columns, place)
    all_branch = near_blocks(grad_branch)
    grad_query_pre, key_parts, value_parts = attention_backward(flags, *back)
    far_keys, *moved = together(key_parts[3], *columns, *all_branch)
    columns, all_branch = moved[:4], moved[4:]
    key_parts = (*key_parts[:3], far_keys, key_parts[4])
    grad_query_pre = grad_query_pre[:, :width]
    back_query = right_inner(grad_query_pre, weights_in[:, :width])
    pack_slot = jnp.sum(pack_slots.astype(F32), axis=0).astype(BF)
    meanwhile = (pack_slot, shift(pack_slot, "zh", 1), back_query, *near_blocks(grad_query_pre))
    grad_kv, pack_slot, pack_other, back_query, *all_query = context_scatter(
        key_parts, value_parts, tables, meanwhile
    )
    pack_slot = add_low(pack_slot, pack_other)
    pack_all = lax.all_gather(pack_slot[None], ("x", "y"), axis=0, tiled=True)
    late = near_blocks(grad_kv)
    y_near, y_far, grad_kv = together(y_near, y_far, grad_kv)
    near = add_low(y_near, shift(y_far, "zl", 1))
    mlp_term = near[0].astype(F32) + shift(near[1], "co", 1).astype(F32)
    result = (middle + mlp_term).astype(BF)[None]
    grad_normed_one = back_query + right_inner(grad_kv, weights_in[:, width:])
    inputs = tokens[0].astype(F32)
    inverse_one = norm_forward(inputs, gains[0])[1]
    through_one, grad_gain_one = norm_backward(inputs, inverse_one, gains[0], grad_normed_one)
    input_grad = (grad_middle + through_one)[None]

    grad_gains = jnp.stack([grad_gain_one, grad_gain_two[0]]).reshape(2, 4, 1, quarter)
    gain_parts = [
        lax.dynamic_index_in_dim(grad_gains, place ^ mask, axis=1, keepdims=False) for mask in range(4)
    ]
    near_gains = jnp.stack(gain_parts[:2]) + shift(jnp.stack(gain_parts[2:]), "zl", 1)
    gains_row = (near_gains[0] + shift(near_gains[1], "co", 1)).reshape(1, 2 * quarter)
    last = weight_gradients(columns, all_branch, all_query, late, jnp.pad(gains_row, ((0, 0), (0, 512 - 2 * quarter))))
    out = slot_sum(last.reshape(16, 16, -1), ("x", "y")).astype(BF)
    out = add_low(out, shift(out, "zh", 1))
    hidden = w_gate.shape[1]
    out, pack_all = together(out, pack_all)
    gate_sum, up_sum, down_sum, done = call(
        unpack_kernel,
        "unpack",
        (((width, hidden), F32), ((width, hidden), F32), ((width, hidden), F32), ((8, 128), F32)),
        pack_all, room=24,
    )
    sum_last = slot_gather(out, ("x", "y")).reshape(256, -1)

    out_sum, query_sum, key_sum, value_sum, gain_sum = call(
        unpack_last_kernel,
        "unpack_last",
        (((quarter, width), F32),) * 2 + (((kv_width, quarter), F32),) * 2 + (((16, 512), F32),),
        sum_last, done, room=16,
    )
    return (
        result,
        input_grad,
        query_sum,
        key_sum.T,
        value_sum.T,
        out_sum,
        gain_sum[0, :quarter],
        gain_sum[0, quarter : 2 * quarter],
        gate_sum,
        up_sum,
        down_sum.T,
    )


def solution(mesh):
    split = Mesh(mesh.devices.reshape(2, 4, 4, 2, 2), ("zh", "x", "y", "zl", "co"))
    ctx = ("zh", "x", "y")
    in_specs = (
        P(FS, ctx, None),
        P(FS, None),
        P(FS, None),
        P(FS, None),
        P(FS, None),
        P(FS, None),
        P(FS),
        P(FS),
        P(None, FS),
        P(None, FS),
        P(FS, None),
        P(FS, ctx, None),
    )
    out_specs = (
        P(FS, ctx, None),
        P(FS, ctx, None),
        P(FS, None),
        P(FS, None),
        P(FS, None),
        P(FS, None),
        P(FS),
        P(FS),
        P(None, FS),
        P(None, FS),
        P(FS, None),
    )
    return jax.shard_map(body, mesh=split, in_specs=in_specs, out_specs=out_specs, check_vma=False)
```
